32 devices in a mesh: groups: 2 (over y), expert: 8 (over z, core), dp: 2 (over x).
Axes of the slice: x: 2, y: 2, z: 4, core: 2. Of those that a mesh axis runs over, the one named last changes fastest.
Arguments:
- tokens: bfloat16 [256, 4096], P(('groups', 'expert', 'dp')), parts along dimension 0, may hold values from -6 to 6
- expert_ids: int32 [256, 8], P(('groups', 'expert', 'dp')), parts along dimension 0, may hold values from 0 to 15, all different within a row; in each aligned block of 8 rows (0 to 7, 8 to 15, ...) at most 8 rows name the same one
- gate_codes: bfloat16 [16, 4096, 1536], P('expert', None, 'dp'), may hold values from -8 to 7, as said below
- up_codes: bfloat16 [16, 4096, 1536], P('expert', None, 'dp'), may hold values from -8 to 7, as said below
- gate_scales: float32 [16, 32, 1536], P('expert', None, 'dp'), may hold values from 0.0015 to 0.006
- up_scales: float32 [16, 32, 1536], P('expert', None, 'dp'), may hold values from 0.0015 to 0.006
Outputs:
- hessian: float32 [32, 1536, 1536], P(('groups', 'expert'), 'dp'), parts along dimension 0
The draws below stay inside these ranges and needn't reach their ends.
There are 2 independent parts, one for each index of `groups`. The reference program is written for one: setup_inputs(seed, part) draws one part's arguments, and reference() takes and returns one part's arrays. A program takes and returns all parts, laid end to end along the dimension named above; an argument that names none is the same for every part. Nothing has to cross between parts.
Inputs may be any that keep to these rules, and one draw needn't show every extreme that they name: `expert_ids`: each token names 8 different experts, every expert is named by some token; among the tokens of one device no expert is named more than 8 times, and some device names some expert exactly 8 times. `gate_codes`: whole numbers. `up_codes`: whole numbers.
All inputs are finite; a program needn't handle non-finite values.
Results may differ from the reference program's by a relative error of at most 0.0071.
Values may be sent and summed in bfloat16 or wider, within the bound.
No kernel may reach another device: no remote copies, remote signals or barrier semaphores. Data moves between devices by JAX's collectives and lax.ppermute only.
A program may use at most 128 MiB of HBM per device.

```python
import math
import jax
import jax.numpy as jnp
import numpy as np
from jax import lax

D = 4096
FF = 1536
TOP = 8
GROUP = 128
TOK_DEV = 8
EXPERTS = 16
TOKENS = 128
CAP = 8
N_EXPERT = 8
N_DP = 2


def draw_gate_codes(key, part):
    key = jax.random.fold_in(key, 11)
    return jax.random.randint(key, (EXPERTS, D, FF), -8, 8).astype(jnp.bfloat16)


def draw_up_codes(key, part):
    key = jax.random.fold_in(key, 12)
    return jax.random.randint(key, (EXPERTS, D, FF), -8, 8).astype(jnp.bfloat16)


def shard_levels(key, dims, shards, smallest, largest):
    level = 1.0
    for axis_at, blocks in shards:
        steps = jax.random.uniform(jax.random.fold_in(jax.random.fold_in(key, 6), axis_at), (blocks,), jnp.float32, smallest / len(shards), largest / len(shards))
        level = level * jnp.repeat(jnp.exp(steps), dims[axis_at] // blocks).reshape((-1,) + (1,) * (len(dims) - 1 - axis_at))
    return level


def deal_out(stream_key, own, number, rows, amount, top, most, lean):
    sequence = jax.random.permutation(stream_key, amount)
    crowded, ordinary = shares(amount, rows * top, most, lean, True), shares(amount, rows * top, most, lean, False)
    places = jnp.arange(amount)

    def named(lengths, rotation):
        used = int((lengths > 0).sum())
        fixed = max(1, used // 4)
        moved = fixed + (places - fixed + rotation * (used - fixed)) % max(1, amount - fixed)
        return jnp.zeros((amount,), jnp.int32).at[sequence[jnp.where(places < fixed, places, moved)]].set(jnp.asarray(lengths, jnp.int32))

    lengths = jnp.where(number % 4 == 0, named(crowded, number // 4), named(ordinary, number - number // 4 - 1))
    mixed = jax.random.permutation(jax.random.fold_in(own, 3), amount)
    donor, receiver = mixed[0:amount // 2 * 2:2], mixed[1:amount // 2 * 2:2]
    room = jnp.minimum(lengths[donor] - 1, most - lengths[receiver]) // 2
    room = jnp.where((donor == sequence[0]) | (receiver == sequence[0]) | (lengths[receiver] == 0), 0, jnp.maximum(room, 0))
    moved = jax.random.randint(jax.random.fold_in(own, 4), (amount // 2,), 0, 1 << 20) % (room + 1)
    lengths = lengths.at[donor].add(-moved).at[receiver].add(moved)
    members = jnp.searchsorted(jnp.cumsum(lengths), jnp.arange(rows * top), side="right").astype(jnp.int32)
    listing = members.reshape(top, rows).T
    listing = listing[jax.random.permutation(jax.random.fold_in(own, 1), rows)]
    rotation = jax.random.randint(jax.random.fold_in(own, 2), (rows, 1), 0, top)
    return jnp.take_along_axis(listing, (jnp.arange(top)[None, :] + rotation) % top, axis=1)


def shares(number_of, total, most, skew, full):
    portions = [(1 << 20) // math.isqrt(rank ** skew) + 1 for rank in range(1, number_of + 1)]
    largest = most if full else min(most, max(-(-total // number_of), total * portions[0] // sum(portions)))
    least = 1 if total - largest >= number_of - 1 else 0
    given, rest = [largest] + [least] * (number_of - 1), total - largest - least * (number_of - 1)
    while rest > 0:
        free = [i for i in range(1, number_of) if given[i] < largest] or [i for i in range(1, number_of) if given[i] < most]
        whole, remaining = sum([portions[i] for i in free]), rest
        for i in free:
            extra = min(most - given[i], max(1, remaining * portions[i] // whole), rest)
            given[i] = given[i] + extra
            rest = rest - extra
    return np.array(given)


def normal_values(key, shape, spread, most, split=(), held_as=jnp.bfloat16):
    factor_of = shard_levels(key, shape, split, -0.22, 0.18) if split else 1.0
    entries = jax.random.normal(key, shape, jnp.float32) * spread * factor_of
    return jnp.minimum(jnp.maximum(entries, -most), most).astype(held_as)


def setup_inputs(seed: int = 0, part: int = 0) -> dict:
    key_list = jax.random.split(jax.random.key(seed), 7)
    own_keys = jax.random.split(jax.random.fold_in(key_list[6], part), 7)
    tokens = normal_values(own_keys[0], (TOKENS, D), 1.0, 6.0, ((0, 16),))
    expert_ids_keys = jax.random.split(jax.random.fold_in(own_keys[1], 1), TOKENS // TOK_DEV)
    expert_ids_turns = jax.random.permutation(jax.random.fold_in(own_keys[1], 3), TOKENS // TOK_DEV)
    expert_ids = jax.vmap(lambda own, number: deal_out(jax.random.fold_in(own_keys[1], 2), own, number, TOK_DEV, EXPERTS, TOP, CAP, 1))(expert_ids_keys, expert_ids_turns).reshape((TOKENS, TOP))
    gate_codes = draw_gate_codes(jax.random.fold_in(key_list[6], 71), part)
    up_codes = draw_up_codes(jax.random.fold_in(key_list[6], 71), part)
    gate_scales = jnp.clip(jnp.exp(math.log(0.006) - 1.3862944 * jax.random.uniform(key_list[4], (EXPERTS, D // GROUP, FF), jnp.float32) ** shard_levels(key_list[4], (EXPERTS, D // GROUP, FF), ((0, 8), (2, 2)), -0.2, 0.2)), 0.0015, 0.006)
    up_scales = jnp.clip(jnp.exp(math.log(0.006) - 1.3862944 * jax.random.uniform(key_list[5], (EXPERTS, D // GROUP, FF), jnp.float32) ** shard_levels(key_list[5], (EXPERTS, D // GROUP, FF), ((0, 8), (2, 2)), -0.2, 0.2)), 0.0015, 0.006)
    return {"tokens": tokens, "expert_ids": expert_ids, "gate_codes": gate_codes, "up_codes": up_codes, "gate_scales": gate_scales, "up_scales": up_scales}


def dequantize(codes, scales):
    depth, width = codes.shape
    groups = scales.shape[0]
    blocks = codes.reshape(groups, depth // groups, width).astype(jnp.float32) * scales[:, None, :]
    return blocks.astype(jnp.bfloat16).reshape(depth, width)


def reference(tokens, expert_ids, gate_codes, up_codes, gate_scales, up_scales):
    limit = N_EXPERT * N_DP * CAP

    def one_expert(which):
        member = jnp.sum((expert_ids == which).astype(jnp.int32), axis=1)
        order = jnp.argsort(1 - member, stable=True)[:limit]
        picked = tokens[order]
        keep = member[order].astype(jnp.bfloat16)
        w_gate = dequantize(gate_codes[which], gate_scales[which])
        w_up = dequantize(up_codes[which], up_scales[which])
        gate = jnp.dot(picked, w_gate, preferred_element_type=jnp.float32)
        up = jnp.dot(picked, w_up, preferred_element_type=jnp.float32)
        hidden = (jax.nn.silu(gate) * up).astype(jnp.bfloat16) * keep[:, None]
        total = jnp.sum(member).astype(jnp.float32)
        gram = jnp.dot(hidden.T, hidden, preferred_element_type=jnp.float32)
        return gram * (2.0 / total)

    return lax.map(one_expert, jnp.arange(EXPERTS, dtype=jnp.int32))
```

```python
import functools

import jax
import jax.numpy as jnp
from jax import lax
from jax.experimental import pallas as pl
from jax.experimental.pallas import tpu as pltpu
from jax.sharding import PartitionSpec as P

TOP = 8
LANES = 128
CHUNKS = 8
F32 = jnp.float32
BF16 = jnp.bfloat16


def dequantize(codes, scales):
    owned, depth, width = codes.shape
    groups = scales.shape[1]
    blocks = (
        codes.reshape(owned, groups, depth // groups, width).astype(jnp.float32)
        * scales[:, :, None, :]
    )
    return blocks.astype(jnp.bfloat16).reshape(owned, depth, width)


def slot_table(chosen, targets, capacity):
    member = jnp.sum((chosen[..., :, :, None] == targets).astype(jnp.int32), axis=-2)
    before = jnp.cumsum(member, axis=-2) - member
    member_t = jnp.swapaxes(member, -1, -2)
    before_t = jnp.swapaxes(before, -1, -2)
    slots = jnp.arange(capacity, dtype=jnp.int32)
    table = (member_t[..., :, None, :] == 1) & (before_t[..., :, None, :] == slots[:, None])
    return (table.astype(jnp.bfloat16), jnp.sum(member, axis=-2))


def general(tokens, expert_ids, gate_codes, up_codes, gate_scales, up_scales):
    tok_dev, width = tokens.shape
    owned = gate_codes.shape[0]
    owners = lax.axis_size("expert")
    shards = lax.axis_size("dp")
    capacity = min(tok_dev, 2 * tok_dev * TOP // (owned * owners))
    everyone = jnp.arange(owners * owned, dtype=jnp.int32)
    table, tallies = slot_table(expert_ids, everyone, capacity)
    outgoing = jnp.dot(
        table.reshape(owners * owned * capacity, tok_dev),
        tokens,
        preferred_element_type=jnp.float32,
    )
    outgoing = outgoing.astype(jnp.bfloat16).reshape(owners, owned * capacity, width)
    tally_words = tallies.astype(jnp.bfloat16).reshape(owners, owned)
    copies = jnp.broadcast_to(outgoing[:, None], (owners, shards, owned * capacity, width)).reshape(
        owners * shards, owned * capacity, width
    )
    tally_copies = jnp.broadcast_to(tally_words[:, None], (owners, shards, owned)).reshape(
        owners * shards, owned
    )
    received, counted = (
        lax.all_to_all(copies, ("expert", "dp"), split_axis=0, concat_axis=0, tiled=True),
        lax.all_to_all(tally_copies, ("expert", "dp"), split_axis=0, concat_axis=0, tiled=True),
    )
    arrived = received.reshape(received.shape[0], owned, capacity, width)
    totals = jnp.sum(counted.astype(jnp.float32), axis=0)
    w_gate = dequantize(gate_codes, gate_scales)
    w_up = dequantize(up_codes, up_scales)
    gate = jnp.einsum("sjcd,jdh->jsch", arrived, w_gate, preferred_element_type=jnp.float32)
    up = jnp.einsum("sjcd,jdh->jsch", arrived, w_up, preferred_element_type=jnp.float32)
    sources = arrived.shape[0]
    hidden = (
        (jax.nn.silu(gate) * up)
        .astype(jnp.bfloat16)
        .reshape(owned, sources * capacity, w_gate.shape[2])
    )
    gram = jnp.einsum(
        "jrh,jrw->jhw",
        hidden,
        lax.all_gather(hidden, "dp", axis=2, tiled=True),
        preferred_element_type=jnp.float32,
    )
    return gram * (2.0 / totals)[:, None, None]


def shift(x, axis, by):
    n = lax.axis_size(axis)
    return lax.ppermute(x, axis, [(i, (i + by) % n) for i in range(n)])


def swap(x, axis):
    n = lax.axis_size(axis)
    return lax.ppermute(x, axis, [(i, i ^ 1) for i in range(n)])


def gather_tokens(rows):
    owners = lax.axis_size("expert")
    held = jnp.concatenate([rows] + [shift(rows, "expert", by) for by in range(2, owners, 2)])
    held = jnp.concatenate([held, swap(held, "dp")])
    return jnp.concatenate([held, swap(held, "expert")])


def weights_kernel(expert, gate_ref, up_ref, gate_scale_ref, up_scale_ref, w_ref, sems):
    depth = gate_ref.shape[1]
    groups = gate_scale_ref.shape[1]
    step = depth // groups
    rows = depth // CHUNKS
    codes, scales = (gate_ref, up_ref), (gate_scale_ref, up_scale_ref)

    def copy(which, chunk):
        part = pl.ds(chunk * rows, rows)
        return pltpu.make_async_copy(
            codes[which].at[expert, part], w_ref.at[which, part], sems.at[which, chunk]
        )

    for chunk in range(CHUNKS):
        for which in range(2):
            copy(which, chunk).start()
    for chunk in range(CHUNKS):
        for which in range(2):
            copy(which, chunk).wait()

            @pl.loop(0, rows // step)
            def _(i):
                part = pl.ds(pl.multiple_of(chunk * rows + i * step, step), step)
                scale = scales[which][expert, pl.ds(chunk * (rows // step) + i, 1), :]
                w_ref[which, part, :] = (w_ref[which, part, :].astype(F32) * scale).astype(BF16)


def weights(expert, gate_codes, up_codes, gate_scales, up_scales):
    _, depth, width = gate_codes.shape
    return pl.pallas_call(
        functools.partial(weights_kernel, expert),
        in_specs=[pl.BlockSpec(memory_space=pl.ANY)] * 2
        + [pl.BlockSpec(memory_space=pltpu.VMEM)] * 2,
        out_specs=pl.BlockSpec(memory_space=pltpu.VMEM),
        out_shape=pltpu.VMEM((2, depth, width), BF16),
        scratch_shapes=[pltpu.SemaphoreType.DMA((2, CHUNKS))],
        compiler_params=pltpu.CompilerParams(vmem_limit_bytes=8 << 20),
        cost_estimate=pl.CostEstimate(
            flops=2 * depth * width, bytes_accessed=4 * depth * width, transcendentals=0
        ),
    )(gate_codes, up_codes, gate_scales, up_scales)


def hidden_kernel(which_ref, x_ref, w_ref, h_ref, scale_ref):
    depth, width = w_ref.shape[1:]
    named = x_ref[:, depth:].astype(F32) == which_ref[0].astype(F32)
    member = jnp.sum(named.astype(F32), axis=1, keepdims=True)
    scale_ref[...] = jnp.broadcast_to(2.0 / jnp.sum(member, keepdims=True), scale_ref.shape)
    block = 256 if width % 256 == 0 else width
    x = x_ref[:, :depth]
    for at in range(0, width, block):
        cols = pl.ds(at, block)
        gate = jnp.dot(x, w_ref[0, :, cols], preferred_element_type=F32)
        up = jnp.dot(x, w_ref[1, :, cols], preferred_element_type=F32)
        value = gate / (1.0 + jnp.exp(-gate)) * up
        h_ref[:, cols] = jnp.where(member > 0, value, 0.0).astype(BF16)


def hidden_units(which, x, w):
    _, depth, width = w.shape
    rows = x.shape[0]
    return pl.pallas_call(
        hidden_kernel,
        in_specs=[pl.BlockSpec(memory_space=pltpu.SMEM)]
        + [pl.BlockSpec(memory_space=pltpu.VMEM)] * 2,
        out_specs=[pl.BlockSpec(memory_space=pltpu.VMEM)] * 2,
        out_shape=[
            jax.ShapeDtypeStruct((rows, width), BF16),
            jax.ShapeDtypeStruct((8, LANES), F32),
        ],
        compiler_params=pltpu.CompilerParams(vmem_limit_bytes=8 << 20),
        cost_estimate=pl.CostEstimate(
            flops=4 * rows * depth * width,
            bytes_accessed=2 * depth * width,
            transcendentals=rows * width,
        ),
    )(which, x, w)


def gram_kernel(turned, place_ref, scale_ref, left_ref, right_ref, *out_refs):
    del place_ref
    out_ref = out_refs[-1]
    right = right_ref[...]
    if turned:
        step = right.shape[0] // 4
        right = jnp.concatenate([right[at * step : (at + 1) * step] for at in (1, 0, 3, 2)])
    product = lax.dot_general(
        left_ref[...], right, (((0,), (0,)), ((), ())), preferred_element_type=F32
    )
    out_ref[0] = product * scale_ref[0:1, 0:1]


def gram_block(expert, place, scale, left, right, shape, onto=None, turned=False):
    rows, width = left.shape
    block = 384 if width % 384 == 0 else width
    operands = [place, scale, left, right] + ([] if onto is None else [onto])
    return pl.pallas_call(
        functools.partial(gram_kernel, turned),
        grid_spec=pltpu.PrefetchScalarGridSpec(
            num_scalar_prefetch=1,
            grid=(width // block,),
            in_specs=[
                pl.BlockSpec((8, LANES), lambda i, place: (0, 0)),
                pl.BlockSpec((rows, block), lambda i, place: (0, i)),
                pl.BlockSpec((rows, width), lambda i, place: (0, 0)),
            ]
            + ([] if onto is None else [pl.BlockSpec(memory_space=pl.ANY)]),
            out_specs=pl.BlockSpec((1, block, width), lambda i, place: (expert, i, place[0])),
        ),
        out_shape=jax.ShapeDtypeStruct(shape, F32),
        input_output_aliases={} if onto is None else {4: 0},
        compiler_params=pltpu.CompilerParams(vmem_limit_bytes=16 << 20),
        cost_estimate=pl.CostEstimate(
            flops=2 * rows * width * width, bytes_accessed=4 * width * width, transcendentals=0
        ),
    )(*operands)


def paired(tokens, expert_ids, gate_codes, up_codes, gate_scales, up_scales):
    owned, _, width = gate_codes.shape
    me = lax.axis_index("dp")
    mine, theirs = jnp.reshape(me, (1,)), jnp.reshape(1 - me, (1,))
    first = lax.axis_index("expert") * owned
    named = jnp.pad(
        expert_ids.astype(BF16), ((0, 0), (0, LANES - expert_ids.shape[1])), constant_values=-1
    )
    x = gather_tokens(jnp.concatenate([tokens, named], axis=1))
    w = [weights(e, gate_codes, up_codes, gate_scales, up_scales) for e in range(owned)]
    parts = [hidden_units(jnp.reshape(first + e, (1,)), x, w[e]) for e in range(owned)]
    other = [swap(hidden, "dp") for hidden, _ in parts]
    shape = (owned, width, 2 * width)
    out = None
    for e, (hidden, scale) in enumerate(parts):
        out = gram_block(e, mine, scale, hidden, hidden, shape, out)
    for e, (hidden, scale) in enumerate(parts):
        out = gram_block(e, theirs, scale, hidden, other[e], shape, out, turned=True)
    return out


def local(tokens, expert_ids, gate_codes, up_codes, gate_scales, up_scales):
    args = (tokens, expert_ids, gate_codes, up_codes, gate_scales, up_scales)
    owned, depth, width = gate_codes.shape
    fits = (
        lax.axis_size("dp") == 2
        and lax.axis_size("expert") % 2 == 0
        and width % LANES == 0
        and depth % (CHUNKS * gate_scales.shape[1]) == 0
        and gate_scales.shape[1] % CHUNKS == 0
        and expert_ids.shape[1] <= LANES
        and owned * lax.axis_size("expert") <= 256
        and owned * depth * width * 4 <= 32 << 20
    )
    return paired(*args) if fits else general(*args)


def solution(mesh):
    return jax.shard_map(
        local,
        mesh=mesh,
        in_specs=(
            P(("groups", "expert", "dp"), None),
            P(("groups", "expert", "dp"), None),
            P("expert", None, "dp"),
            P("expert", None, "dp"),
            P("expert", None, "dp"),
            P("expert", None, "dp"),
        ),
        out_specs=P(("groups", "expert"), "dp", None),
        check_vma=False,
    )
```

```python
import functools

import jax
import jax.numpy as jnp
from jax import lax
from jax.experimental import pallas as pl
from jax.experimental.pallas import tpu as pltpu
from jax.sharding import PartitionSpec as P

TOP = 8
LANES = 128
CHUNKS = 8
F32 = jnp.float32
BF16 = jnp.bfloat16


def dequantize(codes, scales):
    owned, depth, width = codes.shape
    groups = scales.shape[1]
    blocks = (
        codes.reshape(owned, groups, depth // groups, width).astype(jnp.float32)
        * scales[:, :, None, :]
    )
    return blocks.astype(jnp.bfloat16).reshape(owned, depth, width)


def slot_table(chosen, targets, capacity):
    member = jnp.sum((chosen[..., :, :, None] == targets).astype(jnp.int32), axis=-2)
    before = jnp.cumsum(member, axis=-2) - member
    member_t = jnp.swapaxes(member, -1, -2)
    before_t = jnp.swapaxes(before, -1, -2)
    slots = jnp.arange(capacity, dtype=jnp.int32)
    table = (member_t[..., :, None, :] == 1) & (before_t[..., :, None, :] == slots[:, None])
    return (table.astype(jnp.bfloat16), jnp.sum(member, axis=-2))


def general(tokens, expert_ids, gate_codes, up_codes, gate_scales, up_scales):
    tok_dev, width = tokens.shape
    owned = gate_codes.shape[0]
    owners = lax.axis_size("expert")
    shards = lax.axis_size("dp")
    capacity = min(tok_dev, 2 * tok_dev * TOP // (owned * owners))
    everyone = jnp.arange(owners * owned, dtype=jnp.int32)
    table, tallies = slot_table(expert_ids, everyone, capacity)
    outgoing = jnp.dot(
        table.reshape(owners * owned * capacity, tok_dev),
        tokens,
        preferred_element_type=jnp.float32,
    )
    outgoing = outgoing.astype(jnp.bfloat16).reshape(owners, owned * capacity, width)
    tally_words = tallies.astype(jnp.bfloat16).reshape(owners, owned)
    copies = jnp.broadcast_to(outgoing[:, None], (owners, shards, owned * capacity, width)).reshape(
        owners * shards, owned * capacity, width
    )
    tally_copies = jnp.broadcast_to(tally_words[:, None], (owners, shards, owned)).reshape(
        owners * shards, owned
    )
    received, counted = (
        lax.all_to_all(copies, ("expert", "dp"), split_axis=0, concat_axis=0, tiled=True),
        lax.all_to_all(tally_copies, ("expert", "dp"), split_axis=0, concat_axis=0, tiled=True),
    )
    arrived = received.reshape(received.shape[0], owned, capacity, width)
    totals = jnp.sum(counted.astype(jnp.float32), axis=0)
    w_gate = dequantize(gate_codes, gate_scales)
    w_up = dequantize(up_codes, up_scales)
    gate = jnp.einsum("sjcd,jdh->jsch", arrived, w_gate, preferred_element_type=jnp.float32)
    up = jnp.einsum("sjcd,jdh->jsch", arrived, w_up, preferred_element_type=jnp.float32)
    sources = arrived.shape[0]
    hidden = (
        (jax.nn.silu(gate) * up)
        .astype(jnp.bfloat16)
        .reshape(owned, sources * capacity, w_gate.shape[2])
    )
    gram = jnp.einsum(
        "jrh,jrw->jhw",
        hidden,
        lax.all_gather(hidden, "dp", axis=2, tiled=True),
        preferred_element_type=jnp.float32,
    )
    return gram * (2.0 / totals)[:, None, None]


def shift(x, axis, by):
    n = lax.axis_size(axis)
    return lax.ppermute(x, axis, [(i, (i + by) % n) for i in range(n)])


def swap(x, axis):
    n = lax.axis_size(axis)
    return lax.ppermute(x, axis, [(i, i ^ 1) for i in range(n)])


def gather_tokens(rows, done):
    owners = lax.axis_size("expert")
    held = jnp.concatenate([rows] + [shift(rows, "expert", by) for by in range(2, owners, 2)])
    held, first = lax.optimization_barrier((held, done[0]))
    held = jnp.concatenate([held, swap(held, "dp")])
    held, rest = lax.optimization_barrier((held, done[1:]))
    return jnp.concatenate([held, swap(held, "expert")]), [first, *rest]


def weights_kernel(expert, gate_ref, up_ref, gate_scale_ref, up_scale_ref, w_ref, done_ref, sems):
    depth = gate_ref.shape[1]
    groups = gate_scale_ref.shape[1]
    step = depth // groups
    rows = depth // CHUNKS
    codes, scales = (gate_ref, up_ref), (gate_scale_ref, up_scale_ref)

    def copy(which, chunk):
        part = pl.ds(chunk * rows, rows)
        return pltpu.make_async_copy(
            codes[which].at[expert, part], w_ref.at[which, part], sems.at[which, chunk]
        )

    done_ref[...] = jnp.zeros_like(done_ref)
    for chunk in range(CHUNKS):
        for which in range(2):
            copy(which, chunk).start()
    for chunk in range(CHUNKS):
        for which in range(2):
            copy(which, chunk).wait()

            @pl.loop(0, rows // step)
            def _(i):
                part = pl.ds(pl.multiple_of(chunk * rows + i * step, step), step)
                scale = scales[which][expert, pl.ds(chunk * (rows // step) + i, 1), :]
                w_ref[which, part, :] = (w_ref[which, part, :].astype(F32) * scale).astype(BF16)


def weights(expert, gate_codes, up_codes, gate_scales, up_scales):
    _, depth, width = gate_codes.shape
    gate_codes = pltpu.with_memory_space_constraint(gate_codes, pltpu.HBM)
    up_codes = pltpu.with_memory_space_constraint(up_codes, pltpu.HBM)
    return pl.pallas_call(
        functools.partial(weights_kernel, expert),
        in_specs=[pl.BlockSpec(memory_space=pltpu.HBM)] * 2
        + [pl.BlockSpec(memory_space=pltpu.VMEM)] * 2,
        out_specs=[pl.BlockSpec(memory_space=pltpu.VMEM)] * 2,
        out_shape=[pltpu.VMEM((2, depth, width), BF16), jax.ShapeDtypeStruct((8, LANES), F32)],
        scratch_shapes=[pltpu.SemaphoreType.DMA((2, CHUNKS))],
        compiler_params=pltpu.CompilerParams(vmem_limit_bytes=8 << 20),
        cost_estimate=pl.CostEstimate(
            flops=2 * depth * width, bytes_accessed=4 * depth * width, transcendentals=0
        ),
    )(gate_codes, up_codes, gate_scales, up_scales)


def hidden_kernel(owned, expert, done_ref, x_ref, w_ref, h_ref, scale_ref):
    del done_ref
    depth, width = w_ref.shape[1:]
    which = lax.axis_index("expert") * owned + expert
    named = x_ref[:, depth:].astype(F32) == which.astype(F32)
    member = jnp.sum(named.astype(F32), axis=1, keepdims=True)
    scale_ref[...] = jnp.broadcast_to(2.0 / jnp.sum(member, keepdims=True), scale_ref.shape)
    block = 256 if width % 256 == 0 else width
    x = x_ref[:, :depth]
    for at in range(0, width, block):
        cols = pl.ds(at, block)
        gate = jnp.dot(x, w_ref[0, :, cols], preferred_element_type=F32)
        up = jnp.dot(x, w_ref[1, :, cols], preferred_element_type=F32)
        value = gate / (1.0 + jnp.exp(-gate)) * up
        h_ref[:, cols] = jnp.where(member > 0, value, 0.0).astype(BF16)


def hidden_units(owned, expert, done, x, w):
    _, depth, width = w.shape
    rows = x.shape[0]
    return pl.pallas_call(
        functools.partial(hidden_kernel, owned, expert),
        in_specs=[pl.BlockSpec(memory_space=pltpu.VMEM)] * 3,
        out_specs=[pl.BlockSpec(memory_space=pltpu.VMEM)] * 2,
        out_shape=[
            jax.ShapeDtypeStruct((rows, width), BF16),
            jax.ShapeDtypeStruct((8, LANES), F32),
        ],
        compiler_params=pltpu.CompilerParams(vmem_limit_bytes=8 << 20),
        cost_estimate=pl.CostEstimate(
            flops=4 * rows * depth * width,
            bytes_accessed=2 * depth * width,
            transcendentals=rows * width,
        ),
    )(done, x, w)


def gram_kernel(turned, scale_ref, left_ref, right_ref, *out_refs):
    out_ref = out_refs[-1]
    right = right_ref[...]
    if turned:
        step = right.shape[0] // 4
        right = jnp.concatenate([right[at * step : (at + 1) * step] for at in (1, 0, 3, 2)])
    product = lax.dot_general(
        left_ref[...], right, (((0,), (0,)), ((), ())), preferred_element_type=F32
    )
    out_ref[0] = product * scale_ref[0:1, 0:1]


def gram_block(expert, scale, left, right, shape, onto=None, turned=False):
    rows, width = left.shape
    block = 384 if width % 384 == 0 else width
    operands = [scale, left, right] + ([] if onto is None else [onto])

    def place(i):
        me = lax.axis_index("dp")
        return expert, i, 1 - me if turned else me

    return pl.pallas_call(
        functools.partial(gram_kernel, turned),
        grid=(width // block,),
        in_specs=[
            pl.BlockSpec((8, LANES), lambda i: (0, 0)),
            pl.BlockSpec((rows, block), lambda i: (0, i)),
            pl.BlockSpec((rows, width), lambda i: (0, 0)),
        ]
        + ([] if onto is None else [pl.BlockSpec(memory_space=pl.ANY)]),
        out_specs=pl.BlockSpec((1, block, width), place),
        out_shape=jax.ShapeDtypeStruct(shape, F32),
        input_output_aliases={} if onto is None else {3: 0},
        compiler_params=pltpu.CompilerParams(vmem_limit_bytes=8 << 20),
        cost_estimate=pl.CostEstimate(
            flops=2 * rows * width * width, bytes_accessed=4 * width * width, transcendentals=0
        ),
    )(*operands)


def paired(tokens, expert_ids, gate_codes, up_codes, gate_scales, up_scales):
    owned, _, width = gate_codes.shape
    named = jnp.pad(
        expert_ids.astype(BF16), ((0, 0), (0, LANES - expert_ids.shape[1])), constant_values=-1
    )
    w, done = zip(
        *[weights(e, gate_codes, up_codes, gate_scales, up_scales) for e in range(owned)]
    )
    x, done = gather_tokens(jnp.concatenate([tokens, named], axis=1), done)
    parts = [hidden_units(owned, e, done[e], x, w[e]) for e in range(owned)]
    other = [swap(hidden, "dp") for hidden, _ in parts]
    shape = (owned, width, 2 * width)
    out = None
    for e, (hidden, scale) in enumerate(parts):
        out = gram_block(e, scale, hidden, hidden, shape, out)
    for e, (hidden, scale) in enumerate(parts):
        out = gram_block(e, scale, hidden, other[e], shape, out, turned=True)
    return out


def local(tokens, expert_ids, gate_codes, up_codes, gate_scales, up_scales):
    args = (tokens, expert_ids, gate_codes, up_codes, gate_scales, up_scales)
    owned, depth, width = gate_codes.shape
    fits = (
        lax.axis_size("dp") == 2
        and lax.axis_size("expert") % 2 == 0
        and width % LANES == 0
        and depth % (CHUNKS * gate_scales.shape[1]) == 0
        and gate_scales.shape[1] % CHUNKS == 0
        and expert_ids.shape[1] <= LANES
        and owned * lax.axis_size("expert") <= 256
        and owned * depth * width * 4 <= 32 << 20
    )
    return paired(*args) if fits else general(*args)


def solution(mesh):
    return jax.shard_map(
        local,
        mesh=mesh,
        in_specs=(
            P(("groups", "expert", "dp"), None),
            P(("groups", "expert", "dp"), None),
            P("expert", None, "dp"),
            P("expert", None, "dp"),
            P("expert", None, "dp"),
            P("expert", None, "dp"),
        ),
        out_specs=P(("groups", "expert"), "dp", None),
        check_vma=False,
    )
```

```python
import functools

import jax
import jax.numpy as jnp
from jax import lax
from jax.experimental import pallas as pl
from jax.experimental.pallas import tpu as pltpu
from jax.sharding import PartitionSpec as P

TOP = 8
LANES = 128
HIDDEN_BLOCK = 128
F32 = jnp.float32
BF16 = jnp.bfloat16


def dequantize(codes, scales):
    owned, depth, width = codes.shape
    groups = scales.shape[1]
    blocks = (
        codes.reshape(owned, groups, depth // groups, width).astype(jnp.float32)
        * scales[:, :, None, :]
    )
    return blocks.astype(jnp.bfloat16).reshape(owned, depth, width)


def slot_table(chosen, targets, capacity):
    member = jnp.sum((chosen[..., :, :, None] == targets).astype(jnp.int32), axis=-2)
    before = jnp.cumsum(member, axis=-2) - member
    member_t = jnp.swapaxes(member, -1, -2)
    before_t = jnp.swapaxes(before, -1, -2)
    slots = jnp.arange(capacity, dtype=jnp.int32)
    table = (member_t[..., :, None, :] == 1) & (before_t[..., :, None, :] == slots[:, None])
    return (table.astype(jnp.bfloat16), jnp.sum(member, axis=-2))


def general(tokens, expert_ids, gate_codes, up_codes, gate_scales, up_scales):
    tok_dev, width = tokens.shape
    owned = gate_codes.shape[0]
    owners = lax.axis_size("expert")
    shards = lax.axis_size("dp")
    capacity = min(tok_dev, 2 * tok_dev * TOP // (owned * owners))
    everyone = jnp.arange(owners * owned, dtype=jnp.int32)
    table, tallies = slot_table(expert_ids, everyone, capacity)
    outgoing = jnp.dot(
        table.reshape(owners * owned * capacity, tok_dev),
        tokens,
        preferred_element_type=jnp.float32,
    )
    outgoing = outgoing.astype(jnp.bfloat16).reshape(owners, owned * capacity, width)
    tally_words = tallies.astype(jnp.bfloat16).reshape(owners, owned)
    copies = jnp.broadcast_to(outgoing[:, None], (owners, shards, owned * capacity, width)).reshape(
        owners * shards, owned * capacity, width
    )
    tally_copies = jnp.broadcast_to(tally_words[:, None], (owners, shards, owned)).reshape(
        owners * shards, owned
    )
    received, counted = (
        lax.all_to_all(copies, ("expert", "dp"), split_axis=0, concat_axis=0, tiled=True),
        lax.all_to_all(tally_copies, ("expert", "dp"), split_axis=0, concat_axis=0, tiled=True),
    )
    arrived = received.reshape(received.shape[0], owned, capacity, width)
    totals = jnp.sum(counted.astype(jnp.float32), axis=0)
    w_gate = dequantize(gate_codes, gate_scales)
    w_up = dequantize(up_codes, up_scales)
    gate = jnp.einsum("sjcd,jdh->jsch", arrived, w_gate, preferred_element_type=jnp.float32)
    up = jnp.einsum("sjcd,jdh->jsch", arrived, w_up, preferred_element_type=jnp.float32)
    sources = arrived.shape[0]
    hidden = (
        (jax.nn.silu(gate) * up)
        .astype(jnp.bfloat16)
        .reshape(owned, sources * capacity, w_gate.shape[2])
    )
    gram = jnp.einsum(
        "jrh,jrw->jhw",
        hidden,
        lax.all_gather(hidden, "dp", axis=2, tiled=True),
        preferred_element_type=jnp.float32,
    )
    return gram * (2.0 / totals)[:, None, None]


def shift(x, axis, by):
    n = lax.axis_size(axis)
    return lax.ppermute(x, axis, [(i, (i + by) % n) for i in range(n)])


def swap(x, axis):
    n = lax.axis_size(axis)
    return lax.ppermute(x, axis, [(i, i ^ 1) for i in range(n)])


def label_kernel(rows_ref, ids_ref, out_ref):
    depth = rows_ref.shape[1]
    ids = ids_ref[...].astype(F32).astype(BF16)
    blank = jnp.full((ids.shape[0], LANES - ids.shape[1]), -1, BF16)
    out_ref[:, :depth] = rows_ref[...]
    out_ref[:, depth:] = jnp.concatenate([ids, blank], axis=1)


def label(rows, ids, cost):
    rows = pltpu.with_memory_space_constraint(rows, pltpu.HBM)
    ids = pltpu.with_memory_space_constraint(ids, pltpu.HBM)
    return pl.pallas_call(
        label_kernel,
        out_shape=jax.ShapeDtypeStruct((rows.shape[0], rows.shape[1] + LANES), BF16),
        compiler_params=pltpu.CompilerParams(vmem_limit_bytes=1 << 20),
        cost_estimate=pl.CostEstimate(flops=cost, bytes_accessed=1 << 20, transcendentals=0),
    )(rows, ids)


def join_kernel(done_ref, *refs):
    del done_ref
    parts = [ref[...].astype(F32) for ref in refs[:-1]]
    refs[-1][...] = jnp.concatenate(parts).astype(BF16)


def join(done, parts):
    rows = sum(part.shape[0] for part in parts)
    return pl.pallas_call(
        join_kernel,
        in_specs=[pl.BlockSpec(memory_space=pltpu.VMEM)] * (1 + len(parts)),
        out_specs=pl.BlockSpec(memory_space=pltpu.VMEM),
        out_shape=jax.ShapeDtypeStruct((rows, parts[0].shape[1]), BF16),
        compiler_params=pltpu.CompilerParams(vmem_limit_bytes=1 << 20),
        cost_estimate=pl.CostEstimate(
            flops=0, bytes_accessed=4 * rows * parts[0].shape[1], transcendentals=0
        ),
    )(done, *parts)


def weights_kernel(codes_ref, scale_ref, *refs):
    w_refs, done_ref = refs[:-1], refs[-1]
    owned, depth, _ = codes_ref.shape
    groups = scale_ref.shape[1]
    step = depth // groups
    done_ref[...] = jnp.zeros_like(done_ref)
    for expert in range(owned):

        @pl.loop(0, groups)
        def _(i):
            part = pl.ds(pl.multiple_of(i * step, step), step)
            scale = scale_ref[expert, pl.ds(i, 1), :]
            w_refs[expert][part, :] = (codes_ref[expert, part, :].astype(F32) * scale).astype(BF16)


def weights(codes, scales):
    owned = codes.shape[0]
    return pl.pallas_call(
        weights_kernel,
        in_specs=[pl.BlockSpec(memory_space=pltpu.VMEM)] * 2,
        out_specs=[pl.BlockSpec(memory_space=pltpu.VMEM)] * (owned + 1),
        out_shape=[pltpu.VMEM(codes.shape[1:], BF16)] * owned
        + [jax.ShapeDtypeStruct((8, LANES), F32)],
        compiler_params=pltpu.CompilerParams(vmem_limit_bytes=1 << 20),
        cost_estimate=pl.CostEstimate(
            flops=1 << 33, bytes_accessed=4 * codes.size, transcendentals=0
        ),
    )(codes, scales)


def hidden_kernel(owned, experts, done_ref, mine_ref, theirs_ref, *refs):
    del done_ref
    w_refs, h_ref, count_ref = refs[:-2], refs[-2], refs[-1]
    depth, width = w_refs[0].shape
    block = HIDDEN_BLOCK if width % HIDDEN_BLOCK == 0 else width
    labelled = jnp.concatenate([mine_ref[...], theirs_ref[...]])
    named = labelled[:, depth:].astype(F32)
    x = labelled[:, :depth]
    for at, expert in enumerate(experts):
        which = lax.axis_index("expert") * owned + expert
        member = jnp.sum((named == which.astype(F32)).astype(F32), axis=1, keepdims=True)
        count_ref[at] = jnp.broadcast_to(jnp.sum(member, keepdims=True), count_ref.shape[1:])
        for col in range(0, width, block):
            cols = pl.ds(col, block)
            gate = jnp.dot(x, w_refs[2 * at][:, cols], preferred_element_type=F32)
            up = jnp.dot(x, w_refs[2 * at + 1][:, cols], preferred_element_type=F32)
            value = gate / (1.0 + jnp.exp(-gate)) * up
            h_ref[at, :, cols] = jnp.where(member > 0, value, 0.0).astype(BF16)


def hidden_units(owned, experts, done, x, w):
    depth, width = w[0][0].shape
    flat = [w[e][i] for e in experts for i in range(2)]
    rows = sum(part.shape[0] for part in x)
    return pl.pallas_call(
        functools.partial(hidden_kernel, owned, experts),
        in_specs=[pl.BlockSpec(memory_space=pltpu.VMEM)] * (3 + len(flat)),
        out_specs=[pl.BlockSpec(memory_space=pltpu.VMEM)] * 2,
        out_shape=[
            jax.ShapeDtypeStruct((len(experts), rows, width), BF16),
            jax.ShapeDtypeStruct((len(experts), 8, LANES), F32),
        ],
        compiler_params=pltpu.CompilerParams(vmem_limit_bytes=4 << 20),
        cost_estimate=pl.CostEstimate(
            flops=4 * len(experts) * rows * depth * width,
            bytes_accessed=4 * len(experts) * depth * width,
            transcendentals=len(experts) * rows * width,
        ),
    )(done, *x, *flat)


def gram_kernel(jobs, *refs):
    n = len(jobs)
    blocks = [refs[6 * i : 6 * i + 6] for i in range(n)]
    out_ref, buffer, sems = refs[-3:]
    me = lax.axis_index("dp")
    width = buffer.shape[2]
    half = width // 2
    copies = []
    for i, (expert, first, second, theirs) in enumerate(jobs):
        place = pl.ds(pl.multiple_of((1 - me if theirs else me) * width, LANES), width)
        left_a, left_b, right_a, right_b, count_a, count_b = blocks[i]
        left = jnp.concatenate([left_a[first], left_b[second]])
        if theirs:
            right = jnp.concatenate([right_b[second], right_a[first]])
        else:
            right = jnp.concatenate([right_a[first], right_b[second]])
        scale = 2.0 / (count_a[first, 0:1, 0:1] + count_b[second, 0:1, 0:1])
        for part in range(2):
            rows = pl.ds(part * half, half)
            product = lax.dot_general(
                left[:, part * half : (part + 1) * half],
                right,
                (((0,), (0,)), ((), ())),
                preferred_element_type=F32,
            )
            buffer[i, rows, :] = product * scale
            copy = pltpu.make_async_copy(
                buffer.at[i, rows], out_ref.at[expert, rows, place], sems.at[i, part]
            )
            copy.start()
            copies.append(copy)
    for copy in copies:
        copy.wait()


def gram_blocks(jobs, operands, shape, onto=None):
    width = shape[1]
    n = len(jobs)
    flat = [x for group in operands for x in group]
    return pl.pallas_call(
        functools.partial(gram_kernel, jobs),
        in_specs=[pl.BlockSpec(memory_space=pltpu.VMEM)] * len(flat)
        + ([] if onto is None else [pl.BlockSpec(memory_space=pl.ANY)]),
        out_specs=pl.BlockSpec(memory_space=pl.ANY),
        out_shape=jax.ShapeDtypeStruct(shape, F32),
        input_output_aliases={} if onto is None else {len(flat): 0},
        scratch_shapes=[
            pltpu.VMEM((n, width, width), F32),
            pltpu.SemaphoreType.DMA((n, 2)),
        ],
        compiler_params=pltpu.CompilerParams(vmem_limit_bytes=12 << 20),
        cost_estimate=pl.CostEstimate(
            flops=2 * n * 128 * width * width,
            bytes_accessed=4 * n * width * width,
            transcendentals=0,
        ),
    )(*flat, *([] if onto is None else [onto]))


def paired(tokens, expert_ids, gate_codes, up_codes, gate_scales, up_scales):
    owned, _, width = gate_codes.shape
    owners = lax.axis_size("expert")
    every = tuple(range(owned))
    rows = label(tokens, expert_ids, 1 << 34)
    *w_gate, gate_done = weights(gate_codes, gate_scales)
    near = join(gate_done, [rows] + [shift(rows, "expert", by) for by in range(2, owners, 2)])
    far = swap(near, "dp")
    *w_up, up_done = weights(up_codes, up_scales)
    w = list(zip(w_gate, w_up))
    near = (near, swap(near, "expert"))
    near_hidden, near_count = hidden_units(owned, every, up_done, near, w)
    far, near_count = lax.optimization_barrier((far, near_count))
    far = (far, swap(far, "expert"))
    near_other = swap(near_hidden, "dp")
    far_parts = [hidden_units(owned, (e,), up_done, far, w) for e in every]
    far_other = [swap(hidden, "dp") for hidden, _ in far_parts]
    shape = (owned, width, 2 * width)
    own, other = [], []
    for e in every:
        hidden, count = far_parts[e]
        own.append((near_hidden, hidden, near_hidden, hidden, near_count, count))
        other.append((near_hidden, hidden, near_other, far_other[e], near_count, count))
    last = owned - 1
    jobs = [(e, e, 0, False) for e in every] + [(e, e, 0, True) for e in range(last)]
    out = gram_blocks(jobs, own + other[:last], shape)
    return gram_blocks([(last, last, 0, True)], other[last:], shape, out)


def local(tokens, expert_ids, gate_codes, up_codes, gate_scales, up_scales):
    args = (tokens, expert_ids, gate_codes, up_codes, gate_scales, up_scales)
    owned, depth, width = gate_codes.shape
    fits = (
        lax.axis_size("dp") == 2
        and lax.axis_size("expert") % 2 == 0
        and width % LANES == 0
        and depth % (16 * gate_scales.shape[1]) == 0
        and tokens.shape[0] * (lax.axis_size("expert") // 2) % 16 == 0
        and expert_ids.shape[1] <= LANES
        and owned * lax.axis_size("expert") <= 256
        and owned * depth * width * 4 <= 32 << 20
    )
    return paired(*args) if fits else general(*args)


def solution(mesh):
    return jax.shard_map(
        local,
        mesh=mesh,
        in_specs=(
            P(("groups", "expert", "dp"), None),
            P(("groups", "expert", "dp"), None),
            P("expert", None, "dp"),
            P("expert", None, "dp"),
            P("expert", None, "dp"),
            P("expert", None, "dp"),
        ),
        out_specs=P(("groups", "expert"), "dp", None),
        check_vma=False,
    )
```

```python
import functools

import jax
import jax.numpy as jnp
from jax import lax
from jax.experimental import pallas as pl
from jax.experimental.pallas import tpu as pltpu
from jax.sharding import PartitionSpec as P

TOP = 8
LANES = 128
NEAR_BLOCK = 768
FAR_BLOCK = 128
F32 = jnp.float32
BF16 = jnp.bfloat16


def dequantize(codes, scales):
    owned, depth, width = codes.shape
    groups = scales.shape[1]
    blocks = (
        codes.reshape(owned, groups, depth // groups, width).astype(jnp.float32)
        * scales[:, :, None, :]
    )
    return blocks.astype(jnp.bfloat16).reshape(owned, depth, width)


def slot_table(chosen, targets, capacity):
    member = jnp.sum((chosen[..., :, :, None] == targets).astype(jnp.int32), axis=-2)
    before = jnp.cumsum(member, axis=-2) - member
    member_t = jnp.swapaxes(member, -1, -2)
    before_t = jnp.swapaxes(before, -1, -2)
    slots = jnp.arange(capacity, dtype=jnp.int32)
    table = (member_t[..., :, None, :] == 1) & (before_t[..., :, None, :] == slots[:, None])
    return (table.astype(jnp.bfloat16), jnp.sum(member, axis=-2))


def general(tokens, expert_ids, gate_codes, up_codes, gate_scales, up_scales):
    tok_dev, width = tokens.shape
    owned = gate_codes.shape[0]
    owners = lax.axis_size("expert")
    shards = lax.axis_size("dp")
    capacity = min(tok_dev, 2 * tok_dev * TOP // (owned * owners))
    everyone = jnp.arange(owners * owned, dtype=jnp.int32)
    table, tallies = slot_table(expert_ids, everyone, capacity)
    outgoing = jnp.dot(
        table.reshape(owners * owned * capacity, tok_dev),
        tokens,
        preferred_element_type=jnp.float32,
    )
    outgoing = outgoing.astype(jnp.bfloat16).reshape(owners, owned * capacity, width)
    tally_words = tallies.astype(jnp.bfloat16).reshape(owners, owned)
    copies = jnp.broadcast_to(outgoing[:, None], (owners, shards, owned * capacity, width)).reshape(
        owners * shards, owned * capacity, width
    )
    tally_copies = jnp.broadcast_to(tally_words[:, None], (owners, shards, owned)).reshape(
        owners * shards, owned
    )
    received, counted = (
        lax.all_to_all(copies, ("expert", "dp"), split_axis=0, concat_axis=0, tiled=True),
        lax.all_to_all(tally_copies, ("expert", "dp"), split_axis=0, concat_axis=0, tiled=True),
    )
    arrived = received.reshape(received.shape[0], owned, capacity, width)
    totals = jnp.sum(counted.astype(jnp.float32), axis=0)
    w_gate = dequantize(gate_codes, gate_scales)
    w_up = dequantize(up_codes, up_scales)
    gate = jnp.einsum("sjcd,jdh->jsch", arrived, w_gate, preferred_element_type=jnp.float32)
    up = jnp.einsum("sjcd,jdh->jsch", arrived, w_up, preferred_element_type=jnp.float32)
    sources = arrived.shape[0]
    hidden = (
        (jax.nn.silu(gate) * up)
        .astype(jnp.bfloat16)
        .reshape(owned, sources * capacity, w_gate.shape[2])
    )
    gram = jnp.einsum(
        "jrh,jrw->jhw",
        hidden,
        lax.all_gather(hidden, "dp", axis=2, tiled=True),
        preferred_element_type=jnp.float32,
    )
    return gram * (2.0 / totals)[:, None, None]


def shift(x, axis, by):
    n = lax.axis_size(axis)
    return lax.ppermute(x, axis, [(i, (i + by) % n) for i in range(n)])


def swap(x, axis):
    n = lax.axis_size(axis)
    return lax.ppermute(x, axis, [(i, i ^ 1) for i in range(n)])


def label_kernel(rows_ref, ids_ref, out_ref):
    depth = rows_ref.shape[1]
    ids = ids_ref[...].astype(F32).astype(BF16)
    blank = jnp.full((ids.shape[0], LANES - ids.shape[1]), -1, BF16)
    out_ref[:, :depth] = rows_ref[...]
    out_ref[:, depth:] = jnp.concatenate([ids, blank], axis=1)


def label(rows, ids, cost):
    rows = pltpu.with_memory_space_constraint(rows, pltpu.HBM)
    ids = pltpu.with_memory_space_constraint(ids, pltpu.HBM)
    return pl.pallas_call(
        label_kernel,
        out_shape=jax.ShapeDtypeStruct((rows.shape[0], rows.shape[1] + LANES), BF16),
        compiler_params=pltpu.CompilerParams(vmem_limit_bytes=1 << 20),
        cost_estimate=pl.CostEstimate(flops=cost, bytes_accessed=1 << 20, transcendentals=0),
    )(rows, ids)


def join_kernel(count, *refs):
    parts = [ref[...].astype(F32) for ref in refs[:count]]
    refs[-1][...] = jnp.concatenate(parts).astype(BF16)


def join(parts, after):
    rows = sum(part.shape[0] for part in parts)
    return pl.pallas_call(
        functools.partial(join_kernel, len(parts)),
        in_specs=[pl.BlockSpec(memory_space=pltpu.VMEM)] * (len(parts) + len(after)),
        out_specs=pl.BlockSpec(memory_space=pltpu.VMEM),
        out_shape=jax.ShapeDtypeStruct((rows, parts[0].shape[1]), BF16),
        compiler_params=pltpu.CompilerParams(vmem_limit_bytes=1 << 20),
        cost_estimate=pl.CostEstimate(
            flops=0, bytes_accessed=4 * rows * parts[0].shape[1], transcendentals=0
        ),
    )(*parts, *after)


def weights_kernel(codes_ref, scale_ref, *refs):
    w_refs, done_ref = refs[:-1], refs[-1]
    owned, depth, _ = codes_ref.shape
    groups = scale_ref.shape[1]
    step = depth // groups
    done_ref[...] = jnp.zeros_like(done_ref)
    for expert in range(owned):

        @pl.loop(0, groups)
        def _(i):
            part = pl.ds(pl.multiple_of(i * step, step), step)
            scale = scale_ref[expert, pl.ds(i, 1), :]
            w_refs[expert][part, :] = (codes_ref[expert, part, :].astype(F32) * scale).astype(BF16)


def weights(codes, scales):
    owned = codes.shape[0]
    return pl.pallas_call(
        weights_kernel,
        in_specs=[pl.BlockSpec(memory_space=pltpu.VMEM)] * 2,
        out_specs=[pl.BlockSpec(memory_space=pltpu.VMEM)] * (owned + 1),
        out_shape=[pltpu.VMEM(codes.shape[1:], BF16)] * owned
        + [jax.ShapeDtypeStruct((32, LANES), F32)],
        compiler_params=pltpu.CompilerParams(vmem_limit_bytes=1 << 20),
        cost_estimate=pl.CostEstimate(
            flops=1 << 33, bytes_accessed=4 * codes.size, transcendentals=0
        ),
    )(codes, scales)


def finish(owned, expert, named, gate, up, h_ref, at, cols):
    which = lax.axis_index("expert") * owned + expert
    member = jnp.sum((named == which.astype(F32)).astype(F32), axis=1, keepdims=True)
    value = gate / (1.0 + jnp.exp(-gate)) * up
    h_ref[at, :, cols] = jnp.where(member > 0, value, 0.0).astype(BF16)
    return jnp.sum(member, keepdims=True)


def near_kernel(owned, mine_ref, theirs_ref, codes_ref, scale_ref, *refs):
    gate_refs, h_ref, count_ref = refs[:owned], refs[owned], refs[owned + 1]
    up_refs, x_ref = refs[-owned - 1 : -1], refs[-1]
    _, depth, width = codes_ref.shape
    groups = scale_ref.shape[1]
    step = depth // groups
    several = 2 if groups % 2 == 0 else 1
    labelled = jnp.concatenate([mine_ref[...], theirs_ref[...]])
    named = labelled[:, depth:].astype(F32)
    x_ref[...] = labelled[:, :depth]
    block = NEAR_BLOCK if width % NEAR_BLOCK == 0 else width
    for expert in range(owned):
        for col in range(0, width, block):
            cols = pl.ds(col, block)
            gate = jnp.dot(x_ref[...], gate_refs[expert][:, cols], preferred_element_type=F32)
            up = jnp.zeros(gate.shape, F32)
            for group in range(0, groups, several):
                part = pl.ds(group * step, several * step)
                codes = codes_ref[expert, part, cols].astype(F32).reshape(several, step, block)
                scale = scale_ref[expert, pl.ds(group, several), cols]
                w = (codes * scale[:, None, :]).astype(BF16).reshape(several * step, block)
                up_refs[expert][part, cols] = w
                up = up + jnp.dot(
                    x_ref[:, pl.ds(group * step, several * step)], w, preferred_element_type=F32
                )
            count = finish(owned, expert, named, gate, up, h_ref, expert, cols)
        count_ref[expert] = jnp.broadcast_to(count, count_ref.shape[1:])


def near_units(x, w_gate, up_codes, up_scales):
    owned, depth, width = up_codes.shape
    rows = sum(part.shape[0] for part in x)
    return pl.pallas_call(
        functools.partial(near_kernel, owned),
        in_specs=[pl.BlockSpec(memory_space=pltpu.VMEM)] * (4 + owned),
        out_specs=[pl.BlockSpec(memory_space=pltpu.VMEM)] * (2 + owned),
        out_shape=[
            jax.ShapeDtypeStruct((owned, rows, width), BF16),
            jax.ShapeDtypeStruct((owned, 32, LANES), F32),
        ]
        + [pltpu.VMEM((depth, width), BF16)] * owned,
        scratch_shapes=[pltpu.VMEM((rows, depth), BF16)],
        compiler_params=pltpu.CompilerParams(vmem_limit_bytes=2 << 20),
        cost_estimate=pl.CostEstimate(
            flops=1 << 33, bytes_accessed=4 * owned * depth * width, transcendentals=0
        ),
    )(*x, up_codes, up_scales, *w_gate)


def far_kernel(
    owned, expert, mine_ref, theirs_ref, gate_ref, up_ref, h_ref, count_ref, x_ref
):
    depth, width = gate_ref.shape
    labelled = jnp.concatenate([mine_ref[...], theirs_ref[...]])
    named = labelled[:, depth:].astype(F32)
    x_ref[...] = labelled[:, :depth]
    block = FAR_BLOCK if width % FAR_BLOCK == 0 else width
    for col in range(0, width, block):
        cols = pl.ds(col, block)
        gate = jnp.dot(x_ref[...], gate_ref[:, cols], preferred_element_type=F32)
        up = jnp.dot(x_ref[...], up_ref[:, cols], preferred_element_type=F32)
        count = finish(owned, expert, named, gate, up, h_ref, 0, cols)
    count_ref[0] = jnp.broadcast_to(count, count_ref.shape[1:])


def far_units(owned, expert, x, gate, up):
    depth, width = gate.shape
    rows = sum(part.shape[0] for part in x)
    return pl.pallas_call(
        functools.partial(far_kernel, owned, expert),
        in_specs=[pl.BlockSpec(memory_space=pltpu.VMEM)] * 4,
        out_specs=[pl.BlockSpec(memory_space=pltpu.VMEM)] * 2,
        out_shape=[
            jax.ShapeDtypeStruct((1, rows, width), BF16),
            jax.ShapeDtypeStruct((1, 32, LANES), F32),
        ],
        scratch_shapes=[pltpu.VMEM((rows, depth), BF16)],
        compiler_params=pltpu.CompilerParams(vmem_limit_bytes=2 << 20),
        cost_estimate=pl.CostEstimate(
            flops=4 * rows * depth * width,
            bytes_accessed=4 * depth * width,
            transcendentals=rows * width,
        ),
    )(*x, gate, up)


def gram_kernel(jobs, *refs):
    n = len(jobs)
    blocks = [refs[6 * i : 6 * i + 6] for i in range(n)]
    out_ref, buffer, sems = refs[-3:]
    me = lax.axis_index("dp")
    width = buffer.shape[2]
    half = width // 2
    copies = []
    for i, (expert, first, second, theirs) in enumerate(jobs):
        place = pl.ds(pl.multiple_of((1 - me if theirs else me) * width, LANES), width)
        left_a, left_b, right_a, right_b, count_a, count_b = blocks[i]
        left = jnp.concatenate([left_a[first], left_b[second]])
        if theirs:
            right = jnp.concatenate([right_b[second], right_a[first]])
        else:
            right = jnp.concatenate([right_a[first], right_b[second]])
        scale = 2.0 / (count_a[first, 0:1, 0:1] + count_b[second, 0:1, 0:1])
        for part in range(2):
            rows = pl.ds(part * half, half)
            product = lax.dot_general(
                left[:, part * half : (part + 1) * half],
                right,
                (((0,), (0,)), ((), ())),
                preferred_element_type=F32,
            )
            buffer[i, rows, :] = product * scale
            copy = pltpu.make_async_copy(
                buffer.at[i, rows], out_ref.at[expert, rows, place], sems.at[i, part]
            )
            copy.start()
            copies.append(copy)
    for copy in copies:
        copy.wait()


def gram_blocks(jobs, operands, shape, onto=None):
    width = shape[1]
    n = len(jobs)
    flat = [x for group in operands for x in group]
    return pl.pallas_call(
        functools.partial(gram_kernel, jobs),
        in_specs=[pl.BlockSpec(memory_space=pltpu.VMEM)] * len(flat)
        + ([] if onto is None else [pl.BlockSpec(memory_space=pl.ANY)]),
        out_specs=pl.BlockSpec(memory_space=pl.ANY),
        out_shape=jax.ShapeDtypeStruct(shape, F32),
        input_output_aliases={} if onto is None else {len(flat): 0},
        scratch_shapes=[
            pltpu.VMEM((n, width, width), F32),
            pltpu.SemaphoreType.DMA((n, 2)),
        ],
        compiler_params=pltpu.CompilerParams(vmem_limit_bytes=12 << 20),
        cost_estimate=pl.CostEstimate(
            flops=2 * n * 128 * width * width,
            bytes_accessed=4 * n * width * width,
            transcendentals=0,
        ),
    )(*flat, *([] if onto is None else [onto]))


def paired(tokens, expert_ids, gate_codes, up_codes, gate_scales, up_scales):
    owned, _, width = gate_codes.shape
    owners = lax.axis_size("expert")
    every = tuple(range(owned))
    rows = label(tokens, expert_ids, 1 << 34)
    *w_gate, gate_done = weights(gate_codes, gate_scales)
    far_own = swap(rows, "dp")
    ring = [shift(rows, "expert", by) for by in range(2, owners, 2)]
    near = join([rows] + ring, [far_own, gate_done])
    far_ring = swap(join(ring, [gate_done]), "dp")
    near = (near, swap(near, "expert"))
    near_hidden, near_count, *w_up = near_units(near, w_gate, up_codes, up_scales)
    far = join([far_own, far_ring], [near_count])
    far = (far, swap(far, "expert"))
    near_other = swap(near_hidden, "dp")
    far_parts = [far_units(owned, e, far, w_gate[e], w_up[e]) for e in every]
    far_other = [swap(hidden, "dp") for hidden, _ in far_parts]
    shape = (owned, width, 2 * width)
    own, other = [], []
    for e in every:
        hidden, count = far_parts[e]
        own.append((near_hidden, hidden, near_hidden, hidden, near_count, count))
        other.append((near_hidden, hidden, near_other, far_other[e], near_count, count))
    out = gram_blocks([(e, e, 0, False) for e in every], own, shape)
    for e in every:
        out = gram_blocks([(e, e, 0, True)], other[e : e + 1], shape, out)
    return out


def local(tokens, expert_ids, gate_codes, up_codes, gate_scales, up_scales):
    args = (tokens, expert_ids, gate_codes, up_codes, gate_scales, up_scales)
    owned, depth, width = gate_codes.shape
    fits = (
        lax.axis_size("dp") == 2
        and lax.axis_size("expert") % 2 == 0
        and width % LANES == 0
        and depth % (16 * gate_scales.shape[1]) == 0
        and tokens.shape[0] * (lax.axis_size("expert") // 2) % 16 == 0
        and expert_ids.shape[1] <= LANES
        and owned * lax.axis_size("expert") <= 256
        and owned * depth * width * 4 <= 32 << 20
    )
    return paired(*args) if fits else general(*args)


def solution(mesh):
    return jax.shard_map(
        local,
        mesh=mesh,
        in_specs=(
            P(("groups", "expert", "dp"), None),
            P(("groups", "expert", "dp"), None),
            P("expert", None, "dp"),
            P("expert", None, "dp"),
            P("expert", None, "dp"),
            P("expert", None, "dp"),
        ),
        out_specs=P(("groups", "expert"), "dp", None),
        check_vma=False,
    )
```

```python
import functools

import jax
import jax.numpy as jnp
from jax import lax
from jax.experimental import pallas as pl
from jax.experimental.pallas import tpu as pltpu
from jax.sharding import PartitionSpec as P

TOP = 8
LANES = 128
NEAR_BLOCK = 768
FAR_BLOCK = 128
F32 = jnp.float32
BF16 = jnp.bfloat16


def dequantize(codes, scales):
    owned, depth, width = codes.shape
    groups = scales.shape[1]
    blocks = (
        codes.reshape(owned, groups, depth // groups, width).astype(jnp.float32)
        * scales[:, :, None, :]
    )
    return blocks.astype(jnp.bfloat16).reshape(owned, depth, width)


def slot_table(chosen, targets, capacity):
    member = jnp.sum((chosen[..., :, :, None] == targets).astype(jnp.int32), axis=-2)
    before = jnp.cumsum(member, axis=-2) - member
    member_t = jnp.swapaxes(member, -1, -2)
    before_t = jnp.swapaxes(before, -1, -2)
    slots = jnp.arange(capacity, dtype=jnp.int32)
    table = (member_t[..., :, None, :] == 1) & (before_t[..., :, None, :] == slots[:, None])
    return (table.astype(jnp.bfloat16), jnp.sum(member, axis=-2))


def general(tokens, expert_ids, gate_codes, up_codes, gate_scales, up_scales):
    tok_dev, width = tokens.shape
    owned = gate_codes.shape[0]
    owners = lax.axis_size("expert")
    shards = lax.axis_size("dp")
    capacity = min(tok_dev, 2 * tok_dev * TOP // (owned * owners))
    everyone = jnp.arange(owners * owned, dtype=jnp.int32)
    table, tallies = slot_table(expert_ids, everyone, capacity)
    outgoing = jnp.dot(
        table.reshape(owners * owned * capacity, tok_dev),
        tokens,
        preferred_element_type=jnp.float32,
    )
    outgoing = outgoing.astype(jnp.bfloat16).reshape(owners, owned * capacity, width)
    tally_words = tallies.astype(jnp.bfloat16).reshape(owners, owned)
    copies = jnp.broadcast_to(outgoing[:, None], (owners, shards, owned * capacity, width)).reshape(
        owners * shards, owned * capacity, width
    )
    tally_copies = jnp.broadcast_to(tally_words[:, None], (owners, shards, owned)).reshape(
        owners * shards, owned
    )
    received, counted = (
        lax.all_to_all(copies, ("expert", "dp"), split_axis=0, concat_axis=0, tiled=True),
        lax.all_to_all(tally_copies, ("expert", "dp"), split_axis=0, concat_axis=0, tiled=True),
    )
    arrived = received.reshape(received.shape[0], owned, capacity, width)
    totals = jnp.sum(counted.astype(jnp.float32), axis=0)
    w_gate = dequantize(gate_codes, gate_scales)
    w_up = dequantize(up_codes, up_scales)
    gate = jnp.einsum("sjcd,jdh->jsch", arrived, w_gate, preferred_element_type=jnp.float32)
    up = jnp.einsum("sjcd,jdh->jsch", arrived, w_up, preferred_element_type=jnp.float32)
    sources = arrived.shape[0]
    hidden = (
        (jax.nn.silu(gate) * up)
        .astype(jnp.bfloat16)
        .reshape(owned, sources * capacity, w_gate.shape[2])
    )
    gram = jnp.einsum(
        "jrh,jrw->jhw",
        hidden,
        lax.all_gather(hidden, "dp", axis=2, tiled=True),
        preferred_element_type=jnp.float32,
    )
    return gram * (2.0 / totals)[:, None, None]


def shift(x, axis, by):
    n = lax.axis_size(axis)
    return lax.ppermute(x, axis, [(i, (i + by) % n) for i in range(n)])


def swap(x, axis):
    n = lax.axis_size(axis)
    return lax.ppermute(x, axis, [(i, i ^ 1) for i in range(n)])


def label_kernel(rows_ref, ids_ref, out_ref):
    depth = rows_ref.shape[1]
    ids = ids_ref[...].astype(F32).astype(BF16)
    blank = jnp.full((ids.shape[0], LANES - ids.shape[1]), -1, BF16)
    out_ref[:, :depth] = rows_ref[...]
    out_ref[:, depth:] = jnp.concatenate([ids, blank], axis=1)


def label(rows, ids, cost):
    rows = pltpu.with_memory_space_constraint(rows, pltpu.HBM)
    ids = pltpu.with_memory_space_constraint(ids, pltpu.HBM)
    return pl.pallas_call(
        label_kernel,
        out_shape=jax.ShapeDtypeStruct((rows.shape[0], rows.shape[1] + LANES), BF16),
        compiler_params=pltpu.CompilerParams(vmem_limit_bytes=2 << 20),
        cost_estimate=pl.CostEstimate(flops=cost, bytes_accessed=1 << 20, transcendentals=0),
    )(rows, ids)


def join_kernel(order, kept, *refs):
    outs = refs[len(refs) - 1 - kept :]
    parts = [refs[at][...].astype(F32) for at in order]
    outs[0][...] = jnp.concatenate(parts).astype(BF16)
    if kept:
        outs[1][...] = refs[len(order)][...]


def join(parts, after, order=None, keep=False):
    order = tuple(range(len(parts))) if order is None else order
    rows = sum(part.shape[0] for part in parts)
    shapes = [jax.ShapeDtypeStruct((rows, parts[0].shape[1]), BF16)]
    if keep:
        shapes.append(jax.ShapeDtypeStruct(after[0].shape, BF16))
    made = pl.pallas_call(
        functools.partial(join_kernel, order, int(keep)),
        in_specs=[pl.BlockSpec(memory_space=pltpu.VMEM)] * (len(parts) + len(after)),
        out_specs=[pl.BlockSpec(memory_space=pltpu.VMEM)] * len(shapes),
        out_shape=shapes,
        compiler_params=pltpu.CompilerParams(vmem_limit_bytes=2 << 20),
        cost_estimate=pl.CostEstimate(
            flops=0, bytes_accessed=4 * rows * parts[0].shape[1], transcendentals=0
        ),
    )(*parts, *after)
    return made if keep else made[0]


def weights_kernel(codes_ref, scale_ref, *refs):
    w_refs, done_ref = refs[:-1], refs[-1]
    owned, depth, _ = codes_ref.shape
    groups = scale_ref.shape[1]
    step = depth // groups
    done_ref[...] = jnp.zeros_like(done_ref)
    for expert in range(owned):

        @pl.loop(0, groups)
        def _(i):
            part = pl.ds(pl.multiple_of(i * step, step), step)
            scale = scale_ref[expert, pl.ds(i, 1), :]
            w_refs[expert][part, :] = (codes_ref[expert, part, :].astype(F32) * scale).astype(BF16)


def weights(codes, scales):
    owned = codes.shape[0]
    return pl.pallas_call(
        weights_kernel,
        in_specs=[pl.BlockSpec(memory_space=pltpu.VMEM)] * 2,
        out_specs=[pl.BlockSpec(memory_space=pltpu.VMEM)] * (owned + 1),
        out_shape=[pltpu.VMEM(codes.shape[1:], BF16)] * owned
        + [jax.ShapeDtypeStruct((32, LANES), F32)],
        compiler_params=pltpu.CompilerParams(vmem_limit_bytes=2 << 20),
        cost_estimate=pl.CostEstimate(
            flops=1 << 33, bytes_accessed=4 * codes.size, transcendentals=0
        ),
    )(codes, scales)


def finish(owned, expert, named, gate, up, h_ref, at, cols):
    which = lax.axis_index("expert") * owned + expert
    member = jnp.sum((named == which.astype(F32)).astype(F32), axis=1, keepdims=True)
    value = gate / (1.0 + jnp.exp(-gate)) * up
    h_ref[at, :, cols] = jnp.where(member > 0, value, 0.0).astype(BF16)
    return jnp.sum(member, keepdims=True)


def near_kernel(owned, mine_ref, theirs_ref, codes_ref, scale_ref, *refs):
    gate_refs, h_ref, count_ref = refs[:owned], refs[owned], refs[owned + 1]
    up_refs, x_ref = refs[-owned - 1 : -1], refs[-1]
    _, depth, width = codes_ref.shape
    groups = scale_ref.shape[1]
    step = depth // groups
    several = 2 if groups % 2 == 0 else 1
    labelled = jnp.concatenate([mine_ref[...], theirs_ref[...]])
    named = labelled[:, depth:].astype(F32)
    x_ref[...] = labelled[:, :depth]
    block = NEAR_BLOCK if width % NEAR_BLOCK == 0 else width
    for expert in range(owned):
        for col in range(0, width, block):
            cols = pl.ds(col, block)
            gate = jnp.dot(x_ref[...], gate_refs[expert][:, cols], preferred_element_type=F32)
            up = jnp.zeros(gate.shape, F32)
            for group in range(0, groups, several):
                part = pl.ds(group * step, several * step)
                codes = codes_ref[expert, part, cols].astype(F32).reshape(several, step, block)
                scale = scale_ref[expert, pl.ds(group, several), cols]
                w = (codes * scale[:, None, :]).astype(BF16).reshape(several * step, block)
                up_refs[expert][part, cols] = w
                up = up + jnp.dot(
                    x_ref[:, pl.ds(group * step, several * step)], w, preferred_element_type=F32
                )
            count = finish(owned, expert, named, gate, up, h_ref, expert, cols)
        count_ref[expert] = jnp.broadcast_to(count, count_ref.shape[1:])


def near_units(x, w_gate, up_codes, up_scales):
    owned, depth, width = up_codes.shape
    rows = sum(part.shape[0] for part in x)
    return pl.pallas_call(
        functools.partial(near_kernel, owned),
        in_specs=[pl.BlockSpec(memory_space=pltpu.VMEM)] * (4 + owned),
        out_specs=[pl.BlockSpec(memory_space=pltpu.VMEM)] * (2 + owned),
        out_shape=[
            jax.ShapeDtypeStruct((owned, rows, width), BF16),
            jax.ShapeDtypeStruct((owned, 32, LANES), F32),
        ]
        + [pltpu.VMEM((depth, width), BF16)] * owned,
        scratch_shapes=[pltpu.VMEM((rows, depth), BF16)],
        compiler_params=pltpu.CompilerParams(vmem_limit_bytes=2 << 20),
        cost_estimate=pl.CostEstimate(
            flops=1 << 33, bytes_accessed=4 * owned * depth * width, transcendentals=0
        ),
    )(*x, up_codes, up_scales, *w_gate)


def far_kernel(
    owned, expert, mine_ref, theirs_ref, gate_ref, up_ref, h_ref, count_ref, x_ref
):
    depth, width = gate_ref.shape
    labelled = jnp.concatenate([mine_ref[...], theirs_ref[...]])
    named = labelled[:, depth:].astype(F32)
    x_ref[...] = labelled[:, :depth]
    block = FAR_BLOCK if width % FAR_BLOCK == 0 else width
    for col in range(0, width, block):
        cols = pl.ds(col, block)
        gate = jnp.dot(x_ref[...], gate_ref[:, cols], preferred_element_type=F32)
        up = jnp.dot(x_ref[...], up_ref[:, cols], preferred_element_type=F32)
        count = finish(owned, expert, named, gate, up, h_ref, 0, cols)
    count_ref[0] = jnp.broadcast_to(count, count_ref.shape[1:])


def far_units(owned, expert, x, gate, up):
    depth, width = gate.shape
    rows = sum(part.shape[0] for part in x)
    return pl.pallas_call(
        functools.partial(far_kernel, owned, expert),
        in_specs=[pl.BlockSpec(memory_space=pltpu.VMEM)] * 4,
        out_specs=[pl.BlockSpec(memory_space=pltpu.VMEM)] * 2,
        out_shape=[
            jax.ShapeDtypeStruct((1, rows, width), BF16),
            jax.ShapeDtypeStruct((1, 32, LANES), F32),
        ],
        scratch_shapes=[pltpu.VMEM((rows, depth), BF16)],
        compiler_params=pltpu.CompilerParams(vmem_limit_bytes=2 << 20),
        cost_estimate=pl.CostEstimate(
            flops=4 * rows * depth * width,
            bytes_accessed=4 * depth * width,
            transcendentals=rows * width,
        ),
    )(*x, gate, up)


def gram_kernel(jobs, *refs):
    n = len(jobs)
    blocks = [refs[6 * i : 6 * i + 6] for i in range(n)]
    out_ref, buffer, sems = refs[-3:]
    me = lax.axis_index("dp")
    width = buffer.shape[2]
    half = width // 2
    copies = []
    for i, (expert, first, second, theirs) in enumerate(jobs):
        place = pl.ds(pl.multiple_of((1 - me if theirs else me) * width, LANES), width)
        left_a, left_b, right_a, right_b, count_a, count_b = blocks[i]
        left = jnp.concatenate([left_a[first], left_b[second]])
        if theirs:
            right = jnp.concatenate([right_b[second], right_a[first]])
        else:
            right = jnp.concatenate([right_a[first], right_b[second]])
        scale = 2.0 / (count_a[first, 0:1, 0:1] + count_b[second, 0:1, 0:1])
        for part in range(2):
            rows = pl.ds(part * half, half)
            product = lax.dot_general(
                left[:, part * half : (part + 1) * half],
                right,
                (((0,), (0,)), ((), ())),
                preferred_element_type=F32,
            )
            buffer[i, rows, :] = product * scale
            copy = pltpu.make_async_copy(
                buffer.at[i, rows], out_ref.at[expert, rows, place], sems.at[i, part]
            )
            copy.start()
            copies.append(copy)
    for copy in copies:
        copy.wait()


def gram_blocks(jobs, operands, shape, onto=None):
    width = shape[1]
    n = len(jobs)
    flat = [x for group in operands for x in group]
    return pl.pallas_call(
        functools.partial(gram_kernel, jobs),
        in_specs=[pl.BlockSpec(memory_space=pltpu.VMEM)] * len(flat)
        + ([] if onto is None else [pl.BlockSpec(memory_space=pl.ANY)]),
        out_specs=pl.BlockSpec(memory_space=pl.ANY),
        out_shape=jax.ShapeDtypeStruct(shape, F32),
        input_output_aliases={} if onto is None else {len(flat): 0},
        scratch_shapes=[
            pltpu.VMEM((n, width, width), F32),
            pltpu.SemaphoreType.DMA((n, 2)),
        ],
        compiler_params=pltpu.CompilerParams(vmem_limit_bytes=8 << 20),
        cost_estimate=pl.CostEstimate(
            flops=2 * n * 128 * width * width,
            bytes_accessed=4 * n * width * width,
            transcendentals=0,
        ),
    )(*flat, *([] if onto is None else [onto]))


def paired(tokens, expert_ids, gate_codes, up_codes, gate_scales, up_scales):
    owned, _, width = gate_codes.shape
    owners = lax.axis_size("expert")
    every = tuple(range(owned))
    rows = label(tokens, expert_ids, 1 << 34)
    *w_gate, gate_done = weights(gate_codes, gate_scales)
    far_own = swap(rows, "dp")
    ring = [shift(rows, "expert", by) for by in range(2, owners, 2)]
    order = (0, *range(2, len(ring) + 1), 1)
    near, far_own = join([rows] + ring, [far_own, gate_done], order, keep=True)
    far_next = shift(far_own, "expert", 2)
    far_ring = swap(join(ring[1:], [ring[0], gate_done]), "dp")
    near = (near, swap(near, "expert"))
    near_hidden, near_count, *w_up = near_units(near, w_gate, up_codes, up_scales)
    far = join([far_own, far_ring, far_next], [near_count])
    far = (far, swap(far, "expert"))
    near_other = swap(near_hidden, "dp")
    far_parts = [far_units(owned, e, far, w_gate[e], w_up[e]) for e in every]
    far_other = [swap(hidden, "dp") for hidden, _ in far_parts]
    shape = (owned, width, 2 * width)
    own, other = [], []
    for e in every:
        hidden, count = far_parts[e]
        own.append((near_hidden, hidden, near_hidden, hidden, near_count, count))
        other.append((near_hidden, hidden, near_other, far_other[e], near_count, count))
    out = gram_blocks([(e, e, 0, False) for e in every], own, shape)
    for e in every:
        out = gram_blocks([(e, e, 0, True)], other[e : e + 1], shape, out)
    return out


def local(tokens, expert_ids, gate_codes, up_codes, gate_scales, up_scales):
    args = (tokens, expert_ids, gate_codes, up_codes, gate_scales, up_scales)
    owned, depth, width = gate_codes.shape
    fits = (
        lax.axis_size("dp") == 2
        and lax.axis_size("expert") % 2 == 0
        and width % LANES == 0
        and depth % (16 * gate_scales.shape[1]) == 0
        and tokens.shape[0] * (lax.axis_size("expert") // 2) % 16 == 0
        and expert_ids.shape[1] <= LANES
        and owned * lax.axis_size("expert") <= 256
        and owned * depth * width * 4 <= 32 << 20
    )
    return paired(*args) if fits else general(*args)


def solution(mesh):
    return jax.shard_map(
        local,
        mesh=mesh,
        in_specs=(
            P(("groups", "expert", "dp"), None),
            P(("groups", "expert", "dp"), None),
            P("expert", None, "dp"),
            P("expert", None, "dp"),
            P("expert", None, "dp"),
            P("expert", None, "dp"),
        ),
        out_specs=P(("groups", "expert"), "dp", None),
        check_vma=False,
    )
```

```python
import functools

import jax
import jax.numpy as jnp
from jax import lax
from jax.experimental import pallas as pl
from jax.experimental.pallas import tpu as pltpu
from jax.sharding import PartitionSpec as P

TOP = 8
LANES = 128
NEAR_BLOCK = 768
FAR_BLOCK = 128
PARTS = 3
F32 = jnp.float32
BF16 = jnp.bfloat16


def dequantize(codes, scales):
    owned, depth, width = codes.shape
    groups = scales.shape[1]
    blocks = (
        codes.reshape(owned, groups, depth // groups, width).astype(jnp.float32)
        * scales[:, :, None, :]
    )
    return blocks.astype(jnp.bfloat16).reshape(owned, depth, width)


def slot_table(chosen, targets, capacity):
    member = jnp.sum((chosen[..., :, :, None] == targets).astype(jnp.int32), axis=-2)
    before = jnp.cumsum(member, axis=-2) - member
    member_t = jnp.swapaxes(member, -1, -2)
    before_t = jnp.swapaxes(before, -1, -2)
    slots = jnp.arange(capacity, dtype=jnp.int32)
    table = (member_t[..., :, None, :] == 1) & (before_t[..., :, None, :] == slots[:, None])
    return (table.astype(jnp.bfloat16), jnp.sum(member, axis=-2))


def general(tokens, expert_ids, gate_codes, up_codes, gate_scales, up_scales):
    tok_dev, width = tokens.shape
    owned = gate_codes.shape[0]
    owners = lax.axis_size("expert")
    shards = lax.axis_size("dp")
    capacity = min(tok_dev, 2 * tok_dev * TOP // (owned * owners))
    everyone = jnp.arange(owners * owned, dtype=jnp.int32)
    table, tallies = slot_table(expert_ids, everyone, capacity)
    outgoing = jnp.dot(
        table.reshape(owners * owned * capacity, tok_dev),
        tokens,
        preferred_element_type=jnp.float32,
    )
    outgoing = outgoing.astype(jnp.bfloat16).reshape(owners, owned * capacity, width)
    tally_words = tallies.astype(jnp.bfloat16).reshape(owners, owned)
    copies = jnp.broadcast_to(outgoing[:, None], (owners, shards, owned * capacity, width)).reshape(
        owners * shards, owned * capacity, width
    )
    tally_copies = jnp.broadcast_to(tally_words[:, None], (owners, shards, owned)).reshape(
        owners * shards, owned
    )
    received, counted = (
        lax.all_to_all(copies, ("expert", "dp"), split_axis=0, concat_axis=0, tiled=True),
        lax.all_to_all(tally_copies, ("expert", "dp"), split_axis=0, concat_axis=0, tiled=True),
    )
    arrived = received.reshape(received.shape[0], owned, capacity, width)
    totals = jnp.sum(counted.astype(jnp.float32), axis=0)
    w_gate = dequantize(gate_codes, gate_scales)
    w_up = dequantize(up_codes, up_scales)
    gate = jnp.einsum("sjcd,jdh->jsch", arrived, w_gate, preferred_element_type=jnp.float32)
    up = jnp.einsum("sjcd,jdh->jsch", arrived, w_up, preferred_element_type=jnp.float32)
    sources = arrived.shape[0]
    hidden = (
        (jax.nn.silu(gate) * up)
        .astype(jnp.bfloat16)
        .reshape(owned, sources * capacity, w_gate.shape[2])
    )
    gram = jnp.einsum(
        "jrh,jrw->jhw",
        hidden,
        lax.all_gather(hidden, "dp", axis=2, tiled=True),
        preferred_element_type=jnp.float32,
    )
    return gram * (2.0 / totals)[:, None, None]


def shift(x, axis, by):
    n = lax.axis_size(axis)
    return lax.ppermute(x, axis, [(i, (i + by) % n) for i in range(n)])


def swap(x, axis):
    n = lax.axis_size(axis)
    return lax.ppermute(x, axis, [(i, i ^ 1) for i in range(n)])


def label_kernel(rows_ref, ids_ref, out_ref):
    depth = rows_ref.shape[1]
    ids = ids_ref[...].astype(F32).astype(BF16)
    blank = jnp.full((ids.shape[0], LANES - ids.shape[1]), -1, BF16)
    out_ref[:, :depth] = rows_ref[...]
    out_ref[:, depth:] = jnp.concatenate([ids, blank], axis=1)


def label(rows, ids, cost):
    rows = pltpu.with_memory_space_constraint(rows, pltpu.HBM)
    ids = pltpu.with_memory_space_constraint(ids, pltpu.HBM)
    return pl.pallas_call(
        label_kernel,
        out_shape=jax.ShapeDtypeStruct((rows.shape[0], rows.shape[1] + LANES), BF16),
        compiler_params=pltpu.CompilerParams(vmem_limit_bytes=2 << 20),
        cost_estimate=pl.CostEstimate(flops=cost, bytes_accessed=1 << 20, transcendentals=0),
    )(rows, ids)


def join_kernel(order, kept, *refs):
    outs = refs[len(refs) - 1 - kept :]
    parts = [refs[at][...].astype(F32) for at in order]
    outs[0][...] = jnp.concatenate(parts).astype(BF16)
    if kept:
        outs[1][...] = refs[len(order)][...]


def join(parts, after, order=None, keep=False):
    order = tuple(range(len(parts))) if order is None else order
    rows = sum(part.shape[0] for part in parts)
    shapes = [jax.ShapeDtypeStruct((rows, parts[0].shape[1]), BF16)]
    if keep:
        shapes.append(jax.ShapeDtypeStruct(after[0].shape, BF16))
    made = pl.pallas_call(
        functools.partial(join_kernel, order, int(keep)),
        in_specs=[pl.BlockSpec(memory_space=pltpu.VMEM)] * (len(parts) + len(after)),
        out_specs=[pl.BlockSpec(memory_space=pltpu.VMEM)] * len(shapes),
        out_shape=shapes,
        compiler_params=pltpu.CompilerParams(vmem_limit_bytes=2 << 20),
        cost_estimate=pl.CostEstimate(
            flops=0, bytes_accessed=4 * rows * parts[0].shape[1], transcendentals=0
        ),
    )(*parts, *after)
    return made if keep else made[0]


def weights_kernel(codes_ref, scale_ref, *refs):
    w_refs, done_ref = refs[:-1], refs[-1]
    owned, depth, _ = codes_ref.shape
    groups = scale_ref.shape[1]
    step = depth // groups
    done_ref[...] = jnp.zeros_like(done_ref)
    for expert in range(owned):

        @pl.loop(0, groups)
        def _(i):
            part = pl.ds(pl.multiple_of(i * step, step), step)
            scale = scale_ref[expert, pl.ds(i, 1), :]
            w_refs[expert][part, :] = (codes_ref[expert, part, :].astype(F32) * scale).astype(BF16)


def weights(codes, scales):
    owned = codes.shape[0]
    return pl.pallas_call(
        weights_kernel,
        in_specs=[pl.BlockSpec(memory_space=pltpu.VMEM)] * 2,
        out_specs=[pl.BlockSpec(memory_space=pltpu.VMEM)] * (owned + 1),
        out_shape=[pltpu.VMEM(codes.shape[1:], BF16)] * owned
        + [jax.ShapeDtypeStruct((16, LANES), F32)],
        compiler_params=pltpu.CompilerParams(vmem_limit_bytes=2 << 20),
        cost_estimate=pl.CostEstimate(
            flops=1 << 33, bytes_accessed=4 * codes.size, transcendentals=0
        ),
    )(codes, scales)


def finish(owned, expert, named, gate, up, h_ref, at, cols):
    which = lax.axis_index("expert") * owned + expert
    member = jnp.sum((named == which.astype(F32)).astype(F32), axis=1, keepdims=True)
    value = gate / (1.0 + jnp.exp(-gate)) * up
    h_ref[at, :, cols] = jnp.where(member > 0, value, 0.0).astype(BF16)
    return jnp.sum(member, keepdims=True)


def near_kernel(owned, mine_ref, theirs_ref, codes_ref, scale_ref, *refs):
    gate_refs, h_ref, count_ref = refs[:owned], refs[owned], refs[owned + 1]
    up_refs, x_ref = refs[-owned - 1 : -1], refs[-1]
    _, depth, width = codes_ref.shape
    groups = scale_ref.shape[1]
    step = depth // groups
    several = 2 if groups % 2 == 0 else 1
    labelled = jnp.concatenate([mine_ref[...], theirs_ref[...]])
    named = labelled[:, depth:].astype(F32)
    x_ref[...] = labelled[:, :depth]
    block = NEAR_BLOCK if width % NEAR_BLOCK == 0 else width
    for expert in range(owned):
        for col in range(0, width, block):
            cols = pl.ds(col, block)
            gate = jnp.dot(x_ref[...], gate_refs[expert][:, cols], preferred_element_type=F32)
            up = jnp.zeros(gate.shape, F32)
            for group in range(0, groups, several):
                part = pl.ds(group * step, several * step)
                codes = codes_ref[expert, part, cols].astype(F32).reshape(several, step, block)
                scale = scale_ref[expert, pl.ds(group, several), cols]
                w = (codes * scale[:, None, :]).astype(BF16).reshape(several * step, block)
                up_refs[expert][part, cols] = w
                up = up + jnp.dot(
                    x_ref[:, pl.ds(group * step, several * step)], w, preferred_element_type=F32
                )
            count = finish(owned, expert, named, gate, up, h_ref, expert, cols)
        count_ref[expert] = jnp.broadcast_to(count, count_ref.shape[1:])


def near_units(x, w_gate, up_codes, up_scales):
    owned, depth, width = up_codes.shape
    rows = sum(part.shape[0] for part in x)
    return pl.pallas_call(
        functools.partial(near_kernel, owned),
        in_specs=[pl.BlockSpec(memory_space=pltpu.VMEM)] * (4 + owned),
        out_specs=[pl.BlockSpec(memory_space=pltpu.VMEM)] * (2 + owned),
        out_shape=[
            jax.ShapeDtypeStruct((owned, rows, width), BF16),
            jax.ShapeDtypeStruct((owned, 32, LANES), F32),
        ]
        + [pltpu.VMEM((depth, width), BF16)] * owned,
        scratch_shapes=[pltpu.VMEM((rows, depth), BF16)],
        compiler_params=pltpu.CompilerParams(vmem_limit_bytes=2 << 20),
        cost_estimate=pl.CostEstimate(
            flops=1 << 33, bytes_accessed=4 * owned * depth * width, transcendentals=0
        ),
    )(*x, up_codes, up_scales, *w_gate)


def far_kernel(
    owned, expert, mine_ref, theirs_ref, gate_ref, up_ref, h_ref, count_ref, x_ref
):
    depth, width = gate_ref.shape
    labelled = jnp.concatenate([mine_ref[...], theirs_ref[...]])
    named = labelled[:, depth:].astype(F32)
    x_ref[...] = labelled[:, :depth]
    block = FAR_BLOCK if width % FAR_BLOCK == 0 else width
    for col in range(0, width, block):
        cols = pl.ds(col, block)
        gate = jnp.dot(x_ref[...], gate_ref[:, cols], preferred_element_type=F32)
        up = jnp.dot(x_ref[...], up_ref[:, cols], preferred_element_type=F32)
        count = finish(owned, expert, named, gate, up, h_ref, 0, cols)
    count_ref[0] = jnp.broadcast_to(count, count_ref.shape[1:])


def far_units(owned, expert, x, gate, up):
    depth, width = gate.shape
    rows = sum(part.shape[0] for part in x)
    return pl.pallas_call(
        functools.partial(far_kernel, owned, expert),
        in_specs=[pl.BlockSpec(memory_space=pltpu.VMEM)] * 4,
        out_specs=[pl.BlockSpec(memory_space=pltpu.VMEM)] * 2,
        out_shape=[
            jax.ShapeDtypeStruct((1, rows, width), BF16),
            jax.ShapeDtypeStruct((1, 32, LANES), F32),
        ],
        scratch_shapes=[pltpu.VMEM((rows, depth), BF16)],
        compiler_params=pltpu.CompilerParams(vmem_limit_bytes=2 << 20),
        cost_estimate=pl.CostEstimate(
            flops=4 * rows * depth * width,
            bytes_accessed=4 * depth * width,
            transcendentals=rows * width,
        ),
    )(*x, gate, up)


def gram_kernel(jobs, *refs):
    n = len(jobs)
    blocks = [refs[6 * i : 6 * i + 6] for i in range(n)]
    out_ref, buffer, sems = refs[-3:]
    me = lax.axis_index("dp")
    width = buffer.shape[2]
    size = width // PARTS
    copies = []
    for i, (expert, first, second, theirs) in enumerate(jobs):
        place = pl.ds(pl.multiple_of((1 - me if theirs else me) * width, LANES), width)
        left_a, left_b, right_a, right_b, count_a, count_b = blocks[i]
        left = jnp.concatenate([left_a[first], left_b[second]])
        if theirs:
            right = jnp.concatenate([right_b[second], right_a[first]])
        else:
            right = jnp.concatenate([right_a[first], right_b[second]])
        scale = 2.0 / (count_a[first, 0:1, 0:1] + count_b[second, 0:1, 0:1])
        for part in range(PARTS):
            rows = pl.ds(part * size, size)
            product = lax.dot_general(
                left[:, part * size : (part + 1) * size],
                right,
                (((0,), (0,)), ((), ())),
                preferred_element_type=F32,
            )
            buffer[i, rows, :] = product * scale
            copy = pltpu.make_async_copy(
                buffer.at[i, rows], out_ref.at[expert, rows, place], sems.at[i, part]
            )
            copy.start()
            copies.append(copy)
    for copy in copies:
        copy.wait()


def gram_blocks(jobs, operands, shape, onto=None):
    width = shape[1]
    n = len(jobs)
    flat = [x for group in operands for x in group]
    return pl.pallas_call(
        functools.partial(gram_kernel, jobs),
        in_specs=[pl.BlockSpec(memory_space=pltpu.VMEM)] * len(flat)
        + ([] if onto is None else [pl.BlockSpec(memory_space=pl.ANY)]),
        out_specs=pl.BlockSpec(memory_space=pl.ANY),
        out_shape=jax.ShapeDtypeStruct(shape, F32),
        input_output_aliases={} if onto is None else {len(flat): 0},
        scratch_shapes=[
            pltpu.VMEM((n, width, width), F32),
            pltpu.SemaphoreType.DMA((n, PARTS)),
        ],
        compiler_params=pltpu.CompilerParams(vmem_limit_bytes=8 << 20),
        cost_estimate=pl.CostEstimate(
            flops=2 * n * 128 * width * width,
            bytes_accessed=4 * n * width * width,
            transcendentals=0,
        ),
    )(*flat, *([] if onto is None else [onto]))


def paired(tokens, expert_ids, gate_codes, up_codes, gate_scales, up_scales):
    owned, _, width = gate_codes.shape
    owners = lax.axis_size("expert")
    every = tuple(range(owned))
    rows = label(tokens, expert_ids, 1 << 34)
    *w_gate, gate_done = weights(gate_codes, gate_scales)
    far_own = swap(rows, "dp")
    ring = [shift(rows, "expert", by) for by in range(2, owners, 2)]
    order = (0, *range(2, len(ring) + 1), 1)
    near, far_own = join([rows] + ring, [far_own, gate_done], order, keep=True)
    far_next = shift(far_own, "expert", 2)
    far_ring = swap(join(ring[1:], [ring[0], gate_done]), "dp")
    near = (near, swap(near, "expert"))
    near_hidden, near_count, *w_up = near_units(near, w_gate, up_codes, up_scales)
    far = join([far_own, far_ring, far_next], [near_count])
    far = (far, swap(far, "expert"))
    near_other = swap(near_hidden, "dp")
    far_parts = [far_units(owned, e, far, w_gate[e], w_up[e]) for e in every]
    far_other = [swap(hidden, "dp") for hidden, _ in far_parts]
    shape = (owned, width, 2 * width)
    own, other = [], []
    for e in every:
        hidden, count = far_parts[e]
        own.append((near_hidden, hidden, near_hidden, hidden, near_count, count))
        other.append((near_hidden, hidden, near_other, far_other[e], near_count, count))
    out = gram_blocks([(e, e, 0, False) for e in every], own, shape)
    for e in every:
        out = gram_blocks([(e, e, 0, True)], other[e : e + 1], shape, out)
    return out


def local(tokens, expert_ids, gate_codes, up_codes, gate_scales, up_scales):
    args = (tokens, expert_ids, gate_codes, up_codes, gate_scales, up_scales)
    owned, depth, width = gate_codes.shape
    fits = (
        lax.axis_size("dp") == 2
        and lax.axis_size("expert") % 2 == 0
        and lax.axis_size("expert") >= 6
        and width % (PARTS * LANES) == 0
        and depth % (16 * gate_scales.shape[1]) == 0
        and tokens.shape[0] * (lax.axis_size("expert") // 2) % 16 == 0
        and expert_ids.shape[1] <= LANES
        and owned * lax.axis_size("expert") <= 256
        and owned * depth * width * 4 <= 32 << 20
    )
    return paired(*args) if fits else general(*args)


def solution(mesh):
    return jax.shard_map(
        local,
        mesh=mesh,
        in_specs=(
            P(("groups", "expert", "dp"), None),
            P(("groups", "expert", "dp"), None),
            P("expert", None, "dp"),
            P("expert", None, "dp"),
            P("expert", None, "dp"),
            P("expert", None, "dp"),
        ),
        out_specs=P(("groups", "expert"), "dp", None),
        check_vma=False,
    )
```

```python
import functools

import jax
import jax.numpy as jnp
from jax import lax
from jax.experimental import pallas as pl
from jax.experimental.pallas import tpu as pltpu
from jax.sharding import PartitionSpec as P

TOP = 8
LANES = 128
NEAR_BLOCK = 768
FAR_BLOCK = 128
PARTS = 3
F32 = jnp.float32
BF16 = jnp.bfloat16


def dequantize(codes, scales):
    owned, depth, width = codes.shape
    groups = scales.shape[1]
    blocks = (
        codes.reshape(owned, groups, depth // groups, width).astype(jnp.float32)
        * scales[:, :, None, :]
    )
    return blocks.astype(jnp.bfloat16).reshape(owned, depth, width)


def slot_table(chosen, targets, capacity):
    member = jnp.sum((chosen[..., :, :, None] == targets).astype(jnp.int32), axis=-2)
    before = jnp.cumsum(member, axis=-2) - member
    member_t = jnp.swapaxes(member, -1, -2)
    before_t = jnp.swapaxes(before, -1, -2)
    slots = jnp.arange(capacity, dtype=jnp.int32)
    table = (member_t[..., :, None, :] == 1) & (before_t[..., :, None, :] == slots[:, None])
    return (table.astype(jnp.bfloat16), jnp.sum(member, axis=-2))


def general(tokens, expert_ids, gate_codes, up_codes, gate_scales, up_scales):
    tok_dev, width = tokens.shape
    owned = gate_codes.shape[0]
    owners = lax.axis_size("expert")
    shards = lax.axis_size("dp")
    capacity = min(tok_dev, 2 * tok_dev * TOP // (owned * owners))
    everyone = jnp.arange(owners * owned, dtype=jnp.int32)
    table, tallies = slot_table(expert_ids, everyone, capacity)
    outgoing = jnp.dot(
        table.reshape(owners * owned * capacity, tok_dev),
        tokens,
        preferred_element_type=jnp.float32,
    )
    outgoing = outgoing.astype(jnp.bfloat16).reshape(owners, owned * capacity, width)
    tally_words = tallies.astype(jnp.bfloat16).reshape(owners, owned)
    copies = jnp.broadcast_to(outgoing[:, None], (owners, shards, owned * capacity, width)).reshape(
        owners * shards, owned * capacity, width
    )
    tally_copies = jnp.broadcast_to(tally_words[:, None], (owners, shards, owned)).reshape(
        owners * shards, owned
    )
    received, counted = (
        lax.all_to_all(copies, ("expert", "dp"), split_axis=0, concat_axis=0, tiled=True),
        lax.all_to_all(tally_copies, ("expert", "dp"), split_axis=0, concat_axis=0, tiled=True),
    )
    arrived = received.reshape(received.shape[0], owned, capacity, width)
    totals = jnp.sum(counted.astype(jnp.float32), axis=0)
    w_gate = dequantize(gate_codes, gate_scales)
    w_up = dequantize(up_codes, up_scales)
    gate = jnp.einsum("sjcd,jdh->jsch", arrived, w_gate, preferred_element_type=jnp.float32)
    up = jnp.einsum("sjcd,jdh->jsch", arrived, w_up, preferred_element_type=jnp.float32)
    sources = arrived.shape[0]
    hidden = (
        (jax.nn.silu(gate) * up)
        .astype(jnp.bfloat16)
        .reshape(owned, sources * capacity, w_gate.shape[2])
    )
    gram = jnp.einsum(
        "jrh,jrw->jhw",
        hidden,
        lax.all_gather(hidden, "dp", axis=2, tiled=True),
        preferred_element_type=jnp.float32,
    )
    return gram * (2.0 / totals)[:, None, None]


def shift(x, axis, by):
    n = lax.axis_size(axis)
    return lax.ppermute(x, axis, [(i, (i + by) % n) for i in range(n)])


def swap(x, axis, by=1):
    n = lax.axis_size(axis)
    return lax.ppermute(x, axis, [(i, i ^ by) for i in range(n)])


def label_kernel(rows_ref, ids_ref, out_ref):
    depth = rows_ref.shape[1]
    ids = ids_ref[...].astype(F32).astype(BF16)
    blank = jnp.full((ids.shape[0], LANES - ids.shape[1]), -1, BF16)
    out_ref[:, :depth] = rows_ref[...]
    out_ref[:, depth:] = jnp.concatenate([ids, blank], axis=1)


def label(rows, ids, cost):
    rows = pltpu.with_memory_space_constraint(rows, pltpu.HBM)
    ids = pltpu.with_memory_space_constraint(ids, pltpu.HBM)
    return pl.pallas_call(
        label_kernel,
        out_shape=jax.ShapeDtypeStruct((rows.shape[0], rows.shape[1] + LANES), BF16),
        compiler_params=pltpu.CompilerParams(vmem_limit_bytes=2 << 20),
        cost_estimate=pl.CostEstimate(flops=cost, bytes_accessed=1 << 20, transcendentals=0),
    )(rows, ids)


def join_kernel(order, kept, *refs):
    outs = refs[-2:] if kept else refs[-1:]
    even = lax.rem(lax.axis_index("expert") // 2, 2) == 0
    parts = []
    for at in order:
        if isinstance(at, tuple):
            parts.append(jnp.where(even, refs[at[0]][...].astype(F32), refs[at[1]][...].astype(F32)))
        else:
            parts.append(refs[at][...].astype(F32))
    outs[0][...] = jnp.concatenate(parts).astype(BF16)
    if kept:
        outs[1][...] = refs[kept][...]


def join(parts, after, order=None, keep=False):
    order = tuple(range(len(parts))) if order is None else order
    rows = sum(parts[at[0] if isinstance(at, tuple) else at].shape[0] for at in order)
    shapes = [jax.ShapeDtypeStruct((rows, parts[0].shape[1]), BF16)]
    if keep:
        shapes.append(jax.ShapeDtypeStruct(after[0].shape, BF16))
    made = pl.pallas_call(
        functools.partial(join_kernel, order, len(parts) if keep else 0),
        in_specs=[pl.BlockSpec(memory_space=pltpu.VMEM)] * (len(parts) + len(after)),
        out_specs=[pl.BlockSpec(memory_space=pltpu.VMEM)] * len(shapes),
        out_shape=shapes,
        compiler_params=pltpu.CompilerParams(vmem_limit_bytes=2 << 20),
        cost_estimate=pl.CostEstimate(
            flops=0, bytes_accessed=4 * rows * parts[0].shape[1], transcendentals=0
        ),
    )(*parts, *after)
    return made if keep else made[0]


def weights_kernel(codes_ref, scale_ref, *refs):
    w_refs, done_ref = refs[:-1], refs[-1]
    owned, depth, _ = codes_ref.shape
    groups = scale_ref.shape[1]
    step = depth // groups
    done_ref[...] = jnp.zeros_like(done_ref)
    for expert in range(owned):

        @pl.loop(0, groups)
        def _(i):
            part = pl.ds(pl.multiple_of(i * step, step), step)
            scale = scale_ref[expert, pl.ds(i, 1), :]
            w_refs[expert][part, :] = (codes_ref[expert, part, :].astype(F32) * scale).astype(BF16)


def weights(codes, scales):
    owned = codes.shape[0]
    return pl.pallas_call(
        weights_kernel,
        in_specs=[pl.BlockSpec(memory_space=pltpu.VMEM)] * 2,
        out_specs=[pl.BlockSpec(memory_space=pltpu.VMEM)] * (owned + 1),
        out_shape=[pltpu.VMEM(codes.shape[1:], BF16)] * owned
        + [jax.ShapeDtypeStruct((16, LANES), F32)],
        compiler_params=pltpu.CompilerParams(vmem_limit_bytes=2 << 20),
        cost_estimate=pl.CostEstimate(
            flops=1 << 33, bytes_accessed=4 * codes.size, transcendentals=0
        ),
    )(codes, scales)


def finish(owned, expert, named, gate, up, h_ref, at, cols):
    which = lax.axis_index("expert") * owned + expert
    member = jnp.sum((named == which.astype(F32)).astype(F32), axis=1, keepdims=True)
    value = gate / (1.0 + jnp.exp(-gate)) * up
    h_ref[at, :, cols] = jnp.where(member > 0, value, 0.0).astype(BF16)
    return jnp.sum(member, keepdims=True)


def near_kernel(owned, mine_ref, theirs_ref, codes_ref, scale_ref, *refs):
    gate_refs, h_ref, count_ref = refs[:owned], refs[owned], refs[owned + 1]
    up_refs, x_ref = refs[-owned - 1 : -1], refs[-1]
    _, depth, width = codes_ref.shape
    groups = scale_ref.shape[1]
    step = depth // groups
    several = 2 if groups % 2 == 0 else 1
    labelled = jnp.concatenate([mine_ref[...], theirs_ref[...]])
    named = labelled[:, depth:].astype(F32)
    x_ref[...] = labelled[:, :depth]
    block = NEAR_BLOCK if width % NEAR_BLOCK == 0 else width
    for expert in range(owned):
        for col in range(0, width, block):
            cols = pl.ds(col, block)
            gate = jnp.dot(x_ref[...], gate_refs[expert][:, cols], preferred_element_type=F32)
            up = jnp.zeros(gate.shape, F32)
            for group in range(0, groups, several):
                part = pl.ds(group * step, several * step)
                codes = codes_ref[expert, part, cols].astype(F32).reshape(several, step, block)
                scale = scale_ref[expert, pl.ds(group, several), cols]
                w = (codes * scale[:, None, :]).astype(BF16).reshape(several * step, block)
                up_refs[expert][part, cols] = w
                up = up + jnp.dot(
                    x_ref[:, pl.ds(group * step, several * step)], w, preferred_element_type=F32
                )
            count = finish(owned, expert, named, gate, up, h_ref, expert, cols)
        count_ref[expert] = jnp.broadcast_to(count, count_ref.shape[1:])


def near_units(x, w_gate, up_codes, up_scales):
    owned, depth, width = up_codes.shape
    rows = sum(part.shape[0] for part in x)
    return pl.pallas_call(
        functools.partial(near_kernel, owned),
        in_specs=[pl.BlockSpec(memory_space=pltpu.VMEM)] * (4 + owned),
        out_specs=[pl.BlockSpec(memory_space=pltpu.VMEM)] * (2 + owned),
        out_shape=[
            jax.ShapeDtypeStruct((owned, rows, width), BF16),
            jax.ShapeDtypeStruct((owned, 32, LANES), F32),
        ]
        + [pltpu.VMEM((depth, width), BF16)] * owned,
        scratch_shapes=[pltpu.VMEM((rows, depth), BF16)],
        compiler_params=pltpu.CompilerParams(vmem_limit_bytes=2 << 20),
        cost_estimate=pl.CostEstimate(
            flops=1 << 33, bytes_accessed=4 * owned * depth * width, transcendentals=0
        ),
    )(*x, up_codes, up_scales, *w_gate)


def far_kernel(
    owned, expert, mine_ref, theirs_ref, gate_ref, up_ref, h_ref, count_ref, x_ref
):
    depth, width = gate_ref.shape
    labelled = jnp.concatenate([mine_ref[...], theirs_ref[...]])
    named = labelled[:, depth:].astype(F32)
    x_ref[...] = labelled[:, :depth]
    block = FAR_BLOCK if width % FAR_BLOCK == 0 else width
    for col in range(0, width, block):
        cols = pl.ds(col, block)
        gate = jnp.dot(x_ref[...], gate_ref[:, cols], preferred_element_type=F32)
        up = jnp.dot(x_ref[...], up_ref[:, cols], preferred_element_type=F32)
        count = finish(owned, expert, named, gate, up, h_ref, 0, cols)
    count_ref[0] = jnp.broadcast_to(count, count_ref.shape[1:])


def far_units(owned, expert, x, gate, up):
    depth, width = gate.shape
    rows = sum(part.shape[0] for part in x)
    return pl.pallas_call(
        functools.partial(far_kernel, owned, expert),
        in_specs=[pl.BlockSpec(memory_space=pltpu.VMEM)] * 4,
        out_specs=[pl.BlockSpec(memory_space=pltpu.VMEM)] * 2,
        out_shape=[
            jax.ShapeDtypeStruct((1, rows, width), BF16),
            jax.ShapeDtypeStruct((1, 32, LANES), F32),
        ],
        scratch_shapes=[pltpu.VMEM((rows, depth), BF16)],
        compiler_params=pltpu.CompilerParams(vmem_limit_bytes=2 << 20),
        cost_estimate=pl.CostEstimate(
            flops=4 * rows * depth * width,
            bytes_accessed=4 * depth * width,
            transcendentals=rows * width,
        ),
    )(*x, gate, up)


def gram_kernel(jobs, *refs):
    n = len(jobs)
    blocks = [refs[6 * i : 6 * i + 6] for i in range(n)]
    out_ref, buffer, sems = refs[-3:]
    me = lax.axis_index("dp")
    width = buffer.shape[2]
    size = width // PARTS
    copies = []
    for i, (expert, first, second, theirs) in enumerate(jobs):
        place = pl.ds(pl.multiple_of((1 - me if theirs else me) * width, LANES), width)
        left_a, left_b, right_a, right_b, count_a, count_b = blocks[i]
        left = jnp.concatenate([left_a[first], left_b[second]])
        if theirs:
            right = jnp.concatenate([right_b[second], right_a[first]])
        else:
            right = jnp.concatenate([right_a[first], right_b[second]])
        scale = 2.0 / (count_a[first, 0:1, 0:1] + count_b[second, 0:1, 0:1])
        for part in range(PARTS):
            rows = pl.ds(part * size, size)
            product = lax.dot_general(
                left[:, part * size : (part + 1) * size],
                right,
                (((0,), (0,)), ((), ())),
                preferred_element_type=F32,
            )
            buffer[i, rows, :] = product * scale
            copy = pltpu.make_async_copy(
                buffer.at[i, rows], out_ref.at[expert, rows, place], sems.at[i, part]
            )
            copy.start()
            copies.append(copy)
    for copy in copies:
        copy.wait()


def gram_blocks(jobs, operands, shape, onto=None):
    width = shape[1]
    n = len(jobs)
    flat = [x for group in operands for x in group]
    return pl.pallas_call(
        functools.partial(gram_kernel, jobs),
        in_specs=[pl.BlockSpec(memory_space=pltpu.VMEM)] * len(flat)
        + ([] if onto is None else [pl.BlockSpec(memory_space=pl.ANY)]),
        out_specs=pl.BlockSpec(memory_space=pl.ANY),
        out_shape=jax.ShapeDtypeStruct(shape, F32),
        input_output_aliases={} if onto is None else {len(flat): 0},
        scratch_shapes=[
            pltpu.VMEM((n, width, width), F32),
            pltpu.SemaphoreType.DMA((n, PARTS)),
        ],
        compiler_params=pltpu.CompilerParams(vmem_limit_bytes=8 << 20),
        cost_estimate=pl.CostEstimate(
            flops=2 * n * 128 * width * width,
            bytes_accessed=4 * n * width * width,
            transcendentals=0,
        ),
    )(*flat, *([] if onto is None else [onto]))


def paired(tokens, expert_ids, gate_codes, up_codes, gate_scales, up_scales):
    owned, _, width = gate_codes.shape
    owners = lax.axis_size("expert")
    every = tuple(range(owned))
    rows = label(tokens, expert_ids, 1 << 34)
    *w_gate, gate_done = weights(gate_codes, gate_scales)
    far_own = swap(rows, "dp")
    ring = [shift(rows, "expert", by) for by in range(2, owners, 2)]
    order = (0, 2, (1, 3), (3, 1))
    near, far_own = join([rows] + ring, [far_own, gate_done], order, keep=True)
    far_ring = swap(join(ring, [gate_done], (1, (0, 2))), "dp")
    near = (near, swap(near, "expert"))
    far_own, held = lax.optimization_barrier((far_own, near[1]))
    far_next = swap(far_own, "expert", 2)
    near = (near[0], held)
    near_hidden, near_count, *w_up = near_units(near, w_gate, up_codes, up_scales)
    far = join([far_own, far_ring, far_next], [near_count])
    far = (far, swap(far, "expert"))
    near_other = swap(near_hidden, "dp")
    far_parts = [far_units(owned, e, far, w_gate[e], w_up[e]) for e in every]
    far_other = [swap(hidden, "dp") for hidden, _ in far_parts]
    shape = (owned, width, 2 * width)
    own, other = [], []
    for e in every:
        hidden, count = far_parts[e]
        own.append((near_hidden, hidden, near_hidden, hidden, near_count, count))
        other.append((near_hidden, hidden, near_other, far_other[e], near_count, count))
    out = gram_blocks([(e, e, 0, False) for e in every], own, shape)
    for e in every:
        out = gram_blocks([(e, e, 0, True)], other[e : e + 1], shape, out)
    return out


def local(tokens, expert_ids, gate_codes, up_codes, gate_scales, up_scales):
    args = (tokens, expert_ids, gate_codes, up_codes, gate_scales, up_scales)
    owned, depth, width = gate_codes.shape
    fits = (
        lax.axis_size("dp") == 2
        and lax.axis_size("expert") == 8
        and width % (PARTS * LANES) == 0
        and depth % (16 * gate_scales.shape[1]) == 0
        and tokens.shape[0] * (lax.axis_size("expert") // 2) % 16 == 0
        and expert_ids.shape[1] <= LANES
        and owned * lax.axis_size("expert") <= 256
        and owned * depth * width * 4 <= 32 << 20
    )
    return paired(*args) if fits else general(*args)


def solution(mesh):
    return jax.shard_map(
        local,
        mesh=mesh,
        in_specs=(
            P(("groups", "expert", "dp"), None),
            P(("groups", "expert", "dp"), None),
            P("expert", None, "dp"),
            P("expert", None, "dp"),
            P("expert", None, "dp"),
            P("expert", None, "dp"),
        ),
        out_specs=P(("groups", "expert"), "dp", None),
        check_vma=False,
    )
```

```python
import functools

import jax
import jax.numpy as jnp
from jax import lax
from jax.experimental import pallas as pl
from jax.experimental.pallas import tpu as pltpu
from jax.sharding import PartitionSpec as P

TOP = 8
LANES = 128
NEAR_BLOCK = 768
FAR_BLOCK = 128
PARTS = 6
F32 = jnp.float32
BF16 = jnp.bfloat16


def dequantize(codes, scales):
    owned, depth, width = codes.shape
    groups = scales.shape[1]
    blocks = (
        codes.reshape(owned, groups, depth // groups, width).astype(jnp.float32)
        * scales[:, :, None, :]
    )
    return blocks.astype(jnp.bfloat16).reshape(owned, depth, width)


def slot_table(chosen, targets, capacity):
    member = jnp.sum((chosen[..., :, :, None] == targets).astype(jnp.int32), axis=-2)
    before = jnp.cumsum(member, axis=-2) - member
    member_t = jnp.swapaxes(member, -1, -2)
    before_t = jnp.swapaxes(before, -1, -2)
    slots = jnp.arange(capacity, dtype=jnp.int32)
    table = (member_t[..., :, None, :] == 1) & (before_t[..., :, None, :] == slots[:, None])
    return (table.astype(jnp.bfloat16), jnp.sum(member, axis=-2))


def general(tokens, expert_ids, gate_codes, up_codes, gate_scales, up_scales):
    tok_dev, width = tokens.shape
    owned = gate_codes.shape[0]
    owners = lax.axis_size("expert")
    shards = lax.axis_size("dp")
    capacity = min(tok_dev, 2 * tok_dev * TOP // (owned * owners))
    everyone = jnp.arange(owners * owned, dtype=jnp.int32)
    table, tallies = slot_table(expert_ids, everyone, capacity)
    outgoing = jnp.dot(
        table.reshape(owners * owned * capacity, tok_dev),
        tokens,
        preferred_element_type=jnp.float32,
    )
    outgoing = outgoing.astype(jnp.bfloat16).reshape(owners, owned * capacity, width)
    tally_words = tallies.astype(jnp.bfloat16).reshape(owners, owned)
    copies = jnp.broadcast_to(outgoing[:, None], (owners, shards, owned * capacity, width)).reshape(
        owners * shards, owned * capacity, width
    )
    tally_copies = jnp.broadcast_to(tally_words[:, None], (owners, shards, owned)).reshape(
        owners * shards, owned
    )
    received, counted = (
        lax.all_to_all(copies, ("expert", "dp"), split_axis=0, concat_axis=0, tiled=True),
        lax.all_to_all(tally_copies, ("expert", "dp"), split_axis=0, concat_axis=0, tiled=True),
    )
    arrived = received.reshape(received.shape[0], owned, capacity, width)
    totals = jnp.sum(counted.astype(jnp.float32), axis=0)
    w_gate = dequantize(gate_codes, gate_scales)
    w_up = dequantize(up_codes, up_scales)
    gate = jnp.einsum("sjcd,jdh->jsch", arrived, w_gate, preferred_element_type=jnp.float32)
    up = jnp.einsum("sjcd,jdh->jsch", arrived, w_up, preferred_element_type=jnp.float32)
    sources = arrived.shape[0]
    hidden = (
        (jax.nn.silu(gate) * up)
        .astype(jnp.bfloat16)
        .reshape(owned, sources * capacity, w_gate.shape[2])
    )
    gram = jnp.einsum(
        "jrh,jrw->jhw",
        hidden,
        lax.all_gather(hidden, "dp", axis=2, tiled=True),
        preferred_element_type=jnp.float32,
    )
    return gram * (2.0 / totals)[:, None, None]


def shift(x, axis, by):
    n = lax.axis_size(axis)
    return lax.ppermute(x, axis, [(i, (i + by) % n) for i in range(n)])


def swap(x, axis, by=1):
    n = lax.axis_size(axis)
    return lax.ppermute(x, axis, [(i, i ^ by) for i in range(n)])


def label_kernel(rows_ref, ids_ref, out_ref):
    depth = rows_ref.shape[1]
    ids = ids_ref[...].astype(F32).astype(BF16)
    blank = jnp.full((ids.shape[0], LANES - ids.shape[1]), -1, BF16)
    out_ref[:, :depth] = rows_ref[...]
    out_ref[:, depth:] = jnp.concatenate([ids, blank], axis=1)


def label(rows, ids, cost):
    rows = pltpu.with_memory_space_constraint(rows, pltpu.HBM)
    ids = pltpu.with_memory_space_constraint(ids, pltpu.HBM)
    return pl.pallas_call(
        label_kernel,
        out_shape=jax.ShapeDtypeStruct((rows.shape[0], rows.shape[1] + LANES), BF16),
        compiler_params=pltpu.CompilerParams(vmem_limit_bytes=2 << 20),
        cost_estimate=pl.CostEstimate(flops=cost, bytes_accessed=1 << 20, transcendentals=0),
    )(rows, ids)


def join_kernel(order, kept, *refs):
    outs = refs[-2:] if kept else refs[-1:]
    even = lax.rem(lax.axis_index("expert") // 2, 2) == 0
    parts = []
    for at in order:
        if isinstance(at, tuple):
            parts.append(jnp.where(even, refs[at[0]][...].astype(F32), refs[at[1]][...].astype(F32)))
        else:
            parts.append(refs[at][...].astype(F32))
    outs[0][...] = jnp.concatenate(parts).astype(BF16)
    if kept:
        outs[1][...] = refs[kept][...]


def join(parts, after, order=None, keep=False):
    order = tuple(range(len(parts))) if order is None else order
    rows = sum(parts[at[0] if isinstance(at, tuple) else at].shape[0] for at in order)
    shapes = [jax.ShapeDtypeStruct((rows, parts[0].shape[1]), BF16)]
    if keep:
        shapes.append(jax.ShapeDtypeStruct(after[0].shape, BF16))
    made = pl.pallas_call(
        functools.partial(join_kernel, order, len(parts) if keep else 0),
        in_specs=[pl.BlockSpec(memory_space=pltpu.VMEM)] * (len(parts) + len(after)),
        out_specs=[pl.BlockSpec(memory_space=pltpu.VMEM)] * len(shapes),
        out_shape=shapes,
        compiler_params=pltpu.CompilerParams(vmem_limit_bytes=2 << 20),
        cost_estimate=pl.CostEstimate(
            flops=0, bytes_accessed=4 * rows * parts[0].shape[1], transcendentals=0
        ),
    )(*parts, *after)
    return made if keep else made[0]


def weights_kernel(codes_ref, scale_ref, *refs):
    w_refs, done_ref = refs[:-1], refs[-1]
    owned, depth, _ = codes_ref.shape
    groups = scale_ref.shape[1]
    step = depth // groups
    done_ref[...] = jnp.zeros_like(done_ref)
    for expert in range(owned):

        @pl.loop(0, groups)
        def _(i):
            part = pl.ds(pl.multiple_of(i * step, step), step)
            scale = scale_ref[expert, pl.ds(i, 1), :]
            w_refs[expert][part, :] = (codes_ref[expert, part, :].astype(F32) * scale).astype(BF16)


def weights(codes, scales):
    owned = codes.shape[0]
    return pl.pallas_call(
        weights_kernel,
        in_specs=[pl.BlockSpec(memory_space=pltpu.VMEM)] * 2,
        out_specs=[pl.BlockSpec(memory_space=pltpu.VMEM)] * (owned + 1),
        out_shape=[pltpu.VMEM(codes.shape[1:], BF16)] * owned
        + [jax.ShapeDtypeStruct((16, LANES), F32)],
        compiler_params=pltpu.CompilerParams(vmem_limit_bytes=2 << 20),
        cost_estimate=pl.CostEstimate(
            flops=1 << 33, bytes_accessed=4 * codes.size, transcendentals=0
        ),
    )(codes, scales)


def finish(owned, expert, named, gate, up, h_ref, at, cols):
    which = lax.axis_index("expert") * owned + expert
    member = jnp.sum((named == which.astype(F32)).astype(F32), axis=1, keepdims=True)
    value = gate / (1.0 + jnp.exp(-gate)) * up
    h_ref[at, :, cols] = jnp.where(member > 0, value, 0.0).astype(BF16)
    return jnp.sum(member, keepdims=True)


def near_kernel(owned, mine_ref, theirs_ref, codes_ref, scale_ref, *refs):
    gate_refs, h_ref, count_ref = refs[:owned], refs[owned], refs[owned + 1]
    up_refs, x_ref = refs[-owned - 1 : -1], refs[-1]
    _, depth, width = codes_ref.shape
    groups = scale_ref.shape[1]
    step = depth // groups
    several = 2 if groups % 2 == 0 else 1
    labelled = jnp.concatenate([mine_ref[...], theirs_ref[...]])
    named = labelled[:, depth:].astype(F32)
    x_ref[...] = labelled[:, :depth]
    block = NEAR_BLOCK if width % NEAR_BLOCK == 0 else width
    for expert in range(owned):
        for col in range(0, width, block):
            cols = pl.ds(col, block)
            gate = jnp.dot(x_ref[...], gate_refs[expert][:, cols], preferred_element_type=F32)
            up = jnp.zeros(gate.shape, F32)
            for group in range(0, groups, several):
                part = pl.ds(group * step, several * step)
                codes = codes_ref[expert, part, cols].astype(F32).reshape(several, step, block)
                scale = scale_ref[expert, pl.ds(group, several), cols]
                w = (codes * scale[:, None, :]).astype(BF16).reshape(several * step, block)
                up_refs[expert][part, cols] = w
                up = up + jnp.dot(
                    x_ref[:, pl.ds(group * step, several * step)], w, preferred_element_type=F32
                )
            count = finish(owned, expert, named, gate, up, h_ref, expert, cols)
        count_ref[expert] = jnp.broadcast_to(count, count_ref.shape[1:])


def near_units(x, w_gate, up_codes, up_scales):
    owned, depth, width = up_codes.shape
    rows = sum(part.shape[0] for part in x)
    return pl.pallas_call(
        functools.partial(near_kernel, owned),
        in_specs=[pl.BlockSpec(memory_space=pltpu.VMEM)] * (4 + owned),
        out_specs=[pl.BlockSpec(memory_space=pltpu.VMEM)] * (2 + owned),
        out_shape=[
            jax.ShapeDtypeStruct((owned, rows, width), BF16),
            jax.ShapeDtypeStruct((owned, 32, LANES), F32),
        ]
        + [pltpu.VMEM((depth, width), BF16)] * owned,
        scratch_shapes=[pltpu.VMEM((rows, depth), BF16)],
        compiler_params=pltpu.CompilerParams(vmem_limit_bytes=2 << 20),
        cost_estimate=pl.CostEstimate(
            flops=1 << 33, bytes_accessed=4 * owned * depth * width, transcendentals=0
        ),
    )(*x, up_codes, up_scales, *w_gate)


def far_kernel(
    owned, expert, mine_ref, theirs_ref, gate_ref, up_ref, h_ref, count_ref, x_ref
):
    depth, width = gate_ref.shape
    labelled = jnp.concatenate([mine_ref[...], theirs_ref[...]])
    named = labelled[:, depth:].astype(F32)
    x_ref[...] = labelled[:, :depth]
    block = FAR_BLOCK if width % FAR_BLOCK == 0 else width
    for col in range(0, width, block):
        cols = pl.ds(col, block)
        gate = jnp.dot(x_ref[...], gate_ref[:, cols], preferred_element_type=F32)
        up = jnp.dot(x_ref[...], up_ref[:, cols], preferred_element_type=F32)
        count = finish(owned, expert, named, gate, up, h_ref, 0, cols)
    count_ref[0] = jnp.broadcast_to(count, count_ref.shape[1:])


def far_units(owned, expert, x, gate, up):
    depth, width = gate.shape
    rows = sum(part.shape[0] for part in x)
    return pl.pallas_call(
        functools.partial(far_kernel, owned, expert),
        in_specs=[pl.BlockSpec(memory_space=pltpu.VMEM)] * 4,
        out_specs=[pl.BlockSpec(memory_space=pltpu.VMEM)] * 2,
        out_shape=[
            jax.ShapeDtypeStruct((1, rows, width), BF16),
            jax.ShapeDtypeStruct((1, 32, LANES), F32),
        ],
        scratch_shapes=[pltpu.VMEM((rows, depth), BF16)],
        compiler_params=pltpu.CompilerParams(vmem_limit_bytes=2 << 20),
        cost_estimate=pl.CostEstimate(
            flops=4 * rows * depth * width,
            bytes_accessed=4 * depth * width,
            transcendentals=rows * width,
        ),
    )(*x, gate, up)


def gram_kernel(jobs, *refs):
    n = len(jobs)
    blocks = [refs[6 * i : 6 * i + 6] for i in range(n)]
    out_ref, buffer, sems = refs[-3:]
    me = lax.axis_index("dp")
    width = buffer.shape[2]
    size = width // PARTS
    copies = []
    for i, (expert, first, second, theirs) in enumerate(jobs):
        place = pl.ds(pl.multiple_of((1 - me if theirs else me) * width, LANES), width)
        left_a, left_b, right_a, right_b, count_a, count_b = blocks[i]
        left = jnp.concatenate([left_a[first], left_b[second]])
        if theirs:
            right = jnp.concatenate([right_b[second], right_a[first]])
        else:
            right = jnp.concatenate([right_a[first], right_b[second]])
        scale = 2.0 / (count_a[first, 0:1, 0:1] + count_b[second, 0:1, 0:1])
        for part in range(PARTS):
            rows = pl.ds(part * size, size)
            product = lax.dot_general(
                left[:, part * size : (part + 1) * size],
                right,
                (((0,), (0,)), ((), ())),
                preferred_element_type=F32,
            )
            buffer[i, rows, :] = product * scale
            copy = pltpu.make_async_copy(
                buffer.at[i, rows], out_ref.at[expert, rows, place], sems.at[i, part]
            )
            copy.start()
            copies.append(copy)
    for copy in copies:
        copy.wait()


def gram_blocks(jobs, operands, shape, onto=None):
    width = shape[1]
    n = len(jobs)
    flat = [x for group in operands for x in group]
    return pl.pallas_call(
        functools.partial(gram_kernel, jobs),
        in_specs=[pl.BlockSpec(memory_space=pltpu.VMEM)] * len(flat)
        + ([] if onto is None else [pl.BlockSpec(memory_space=pl.ANY)]),
        out_specs=pl.BlockSpec(memory_space=pl.ANY),
        out_shape=jax.ShapeDtypeStruct(shape, F32),
        input_output_aliases={} if onto is None else {len(flat): 0},
        scratch_shapes=[
            pltpu.VMEM((n, width, width), F32),
            pltpu.SemaphoreType.DMA((n, PARTS)),
        ],
        compiler_params=pltpu.CompilerParams(vmem_limit_bytes=8 << 20),
        cost_estimate=pl.CostEstimate(
            flops=2 * n * 128 * width * width,
            bytes_accessed=4 * n * width * width,
            transcendentals=0,
        ),
    )(*flat, *([] if onto is None else [onto]))


def paired(tokens, expert_ids, gate_codes, up_codes, gate_scales, up_scales):
    owned, _, width = gate_codes.shape
    owners = lax.axis_size("expert")
    every = tuple(range(owned))
    rows = label(tokens, expert_ids, 1 << 34)
    *w_gate, gate_done = weights(gate_codes, gate_scales)
    far_own = swap(rows, "dp")
    ring = [shift(rows, "expert", by) for by in range(2, owners, 2)]
    order = (0, 2, (1, 3), (3, 1))
    near, far_own = join([rows] + ring, [far_own, gate_done], order, keep=True)
    far_ring = swap(join(ring, [gate_done], (1, (0, 2))), "dp")
    near = (near, swap(near, "expert"))
    far_own, held = lax.optimization_barrier((far_own, near[1]))
    far_next = swap(far_own, "expert", 2)
    near = (near[0], held)
    near_hidden, near_count, *w_up = near_units(near, w_gate, up_codes, up_scales)
    far = join([far_own, far_ring, far_next], [near_count])
    far = (far, swap(far, "expert"))
    near_other = swap(near_hidden, "dp")
    far_parts = [far_units(owned, e, far, w_gate[e], w_up[e]) for e in every]
    far_other = [swap(hidden, "dp") for hidden, _ in far_parts]
    shape = (owned, width, 2 * width)
    own, other = [], []
    for e in every:
        hidden, count = far_parts[e]
        own.append((near_hidden, hidden, near_hidden, hidden, near_count, count))
        other.append((near_hidden, hidden, near_other, far_other[e], near_count, count))
    out = gram_blocks([(e, e, 0, False) for e in every], own, shape)
    for e in every:
        out = gram_blocks([(e, e, 0, True)], other[e : e + 1], shape, out)
    return out


def local(tokens, expert_ids, gate_codes, up_codes, gate_scales, up_scales):
    args = (tokens, expert_ids, gate_codes, up_codes, gate_scales, up_scales)
    owned, depth, width = gate_codes.shape
    fits = (
        lax.axis_size("dp") == 2
        and lax.axis_size("expert") == 8
        and width % (PARTS * LANES) == 0
        and depth % (16 * gate_scales.shape[1]) == 0
        and tokens.shape[0] * (lax.axis_size("expert") // 2) % 16 == 0
        and expert_ids.shape[1] <= LANES
        and owned * lax.axis_size("expert") <= 256
        and owned * depth * width * 4 <= 32 << 20
    )
    return paired(*args) if fits else general(*args)


def solution(mesh):
    return jax.shard_map(
        local,
        mesh=mesh,
        in_specs=(
            P(("groups", "expert", "dp"), None),
            P(("groups", "expert", "dp"), None),
            P("expert", None, "dp"),
            P("expert", None, "dp"),
            P("expert", None, "dp"),
            P("expert", None, "dp"),
        ),
        out_specs=P(("groups", "expert"), "dp", None),
        check_vma=False,
    )
```

```python
import functools

import jax
import jax.numpy as jnp
from jax import lax
from jax.experimental import pallas as pl
from jax.experimental.pallas import tpu as pltpu
from jax.sharding import PartitionSpec as P

TOP = 8
LANES = 128
LABEL = 256
NEAR_BLOCK = 768
FAR_BLOCK = 128
PARTS = 3
F32 = jnp.float32
BF16 = jnp.bfloat16


def dequantize(codes, scales):
    owned, depth, width = codes.shape
    groups = scales.shape[1]
    blocks = (
        codes.reshape(owned, groups, depth // groups, width).astype(jnp.float32)
        * scales[:, :, None, :]
    )
    return blocks.astype(jnp.bfloat16).reshape(owned, depth, width)


def slot_table(chosen, targets, capacity):
    member = jnp.sum((chosen[..., :, :, None] == targets).astype(jnp.int32), axis=-2)
    before = jnp.cumsum(member, axis=-2) - member
    member_t = jnp.swapaxes(member, -1, -2)
    before_t = jnp.swapaxes(before, -1, -2)
    slots = jnp.arange(capacity, dtype=jnp.int32)
    table = (member_t[..., :, None, :] == 1) & (before_t[..., :, None, :] == slots[:, None])
    return (table.astype(jnp.bfloat16), jnp.sum(member, axis=-2))


def general(tokens, expert_ids, gate_codes, up_codes, gate_scales, up_scales):
    tok_dev, width = tokens.shape
    owned = gate_codes.shape[0]
    owners = lax.axis_size("expert")
    shards = lax.axis_size("dp")
    capacity = min(tok_dev, 2 * tok_dev * TOP // (owned * owners))
    everyone = jnp.arange(owners * owned, dtype=jnp.int32)
    table, tallies = slot_table(expert_ids, everyone, capacity)
    outgoing = jnp.dot(
        table.reshape(owners * owned * capacity, tok_dev),
        tokens,
        preferred_element_type=jnp.float32,
    )
    outgoing = outgoing.astype(jnp.bfloat16).reshape(owners, owned * capacity, width)
    tally_words = tallies.astype(jnp.bfloat16).reshape(owners, owned)
    copies = jnp.broadcast_to(outgoing[:, None], (owners, shards, owned * capacity, width)).reshape(
        owners * shards, owned * capacity, width
    )
    tally_copies = jnp.broadcast_to(tally_words[:, None], (owners, shards, owned)).reshape(
        owners * shards, owned
    )
    received, counted = (
        lax.all_to_all(copies, ("expert", "dp"), split_axis=0, concat_axis=0, tiled=True),
        lax.all_to_all(tally_copies, ("expert", "dp"), split_axis=0, concat_axis=0, tiled=True),
    )
    arrived = received.reshape(received.shape[0], owned, capacity, width)
    totals = jnp.sum(counted.astype(jnp.float32), axis=0)
    w_gate = dequantize(gate_codes, gate_scales)
    w_up = dequantize(up_codes, up_scales)
    gate = jnp.einsum("sjcd,jdh->jsch", arrived, w_gate, preferred_element_type=jnp.float32)
    up = jnp.einsum("sjcd,jdh->jsch", arrived, w_up, preferred_element_type=jnp.float32)
    sources = arrived.shape[0]
    hidden = (
        (jax.nn.silu(gate) * up)
        .astype(jnp.bfloat16)
        .reshape(owned, sources * capacity, w_gate.shape[2])
    )
    gram = jnp.einsum(
        "jrh,jrw->jhw",
        hidden,
        lax.all_gather(hidden, "dp", axis=2, tiled=True),
        preferred_element_type=jnp.float32,
    )
    return gram * (2.0 / totals)[:, None, None]


def shift(x, axis, by):
    n = lax.axis_size(axis)
    return lax.ppermute(x, axis, [(i, (i + by) % n) for i in range(n)])


def swap(x, axis, by=1):
    n = lax.axis_size(axis)
    return lax.ppermute(x, axis, [(i, i ^ by) for i in range(n)])


def label_kernel(rows_ref, ids_ref, out_ref):
    depth = rows_ref.shape[1]
    ids = ids_ref[...].astype(F32).astype(BF16)
    blank = jnp.full((ids.shape[0], LABEL - ids.shape[1]), -1, BF16)
    out_ref[:, :depth] = rows_ref[...]
    out_ref[:, depth:] = jnp.concatenate([ids, blank], axis=1)


def label(rows, ids, cost):
    rows = pltpu.with_memory_space_constraint(rows, pltpu.HBM)
    ids = pltpu.with_memory_space_constraint(ids, pltpu.HBM)
    return pl.pallas_call(
        label_kernel,
        out_shape=jax.ShapeDtypeStruct((rows.shape[0], rows.shape[1] + LABEL), BF16),
        compiler_params=pltpu.CompilerParams(vmem_limit_bytes=2 << 20),
        cost_estimate=pl.CostEstimate(flops=cost, bytes_accessed=1 << 20, transcendentals=0),
    )(rows, ids)


def join_kernel(order, kept, *refs):
    outs = refs[-2:] if kept else refs[-1:]
    even = lax.rem(lax.axis_index("expert") // 2, 2) == 0
    parts = []
    for at in order:
        if isinstance(at, tuple):
            parts.append(jnp.where(even, refs[at[0]][...].astype(F32), refs[at[1]][...].astype(F32)))
        else:
            parts.append(refs[at][...].astype(F32))
    outs[0][...] = jnp.concatenate(parts).astype(BF16)
    if kept:
        outs[1][...] = refs[kept][...]


def join(parts, after, order=None, keep=False):
    order = tuple(range(len(parts))) if order is None else order
    rows = sum(parts[at[0] if isinstance(at, tuple) else at].shape[0] for at in order)
    shapes = [jax.ShapeDtypeStruct((rows, parts[0].shape[1]), BF16)]
    if keep:
        shapes.append(jax.ShapeDtypeStruct(after[0].shape, BF16))
    made = pl.pallas_call(
        functools.partial(join_kernel, order, len(parts) if keep else 0),
        in_specs=[pl.BlockSpec(memory_space=pltpu.VMEM)] * (len(parts) + len(after)),
        out_specs=[pl.BlockSpec(memory_space=pltpu.VMEM)] * len(shapes),
        out_shape=shapes,
        compiler_params=pltpu.CompilerParams(vmem_limit_bytes=2 << 20),
        cost_estimate=pl.CostEstimate(
            flops=0, bytes_accessed=4 * rows * parts[0].shape[1], transcendentals=0
        ),
    )(*parts, *after)
    return made if keep else made[0]


def weights_kernel(codes_ref, scale_ref, *refs):
    w_refs, done_ref = refs[:-1], refs[-1]
    owned, depth, _ = codes_ref.shape
    groups = scale_ref.shape[1]
    step = depth // groups
    done_ref[...] = jnp.zeros_like(done_ref)
    for expert in range(owned):

        @pl.loop(0, groups)
        def _(i):
            part = pl.ds(pl.multiple_of(i * step, step), step)
            scale = scale_ref[expert, pl.ds(i, 1), :]
            w_refs[expert][part, :] = (codes_ref[expert, part, :].astype(F32) * scale).astype(BF16)


def weights(codes, scales):
    owned = codes.shape[0]
    return pl.pallas_call(
        weights_kernel,
        in_specs=[pl.BlockSpec(memory_space=pltpu.VMEM)] * 2,
        out_specs=[pl.BlockSpec(memory_space=pltpu.VMEM)] * (owned + 1),
        out_shape=[pltpu.VMEM(codes.shape[1:], BF16)] * owned
        + [jax.ShapeDtypeStruct((16, LANES), F32)],
        compiler_params=pltpu.CompilerParams(vmem_limit_bytes=2 << 20),
        cost_estimate=pl.CostEstimate(
            flops=1 << 33, bytes_accessed=4 * codes.size, transcendentals=0
        ),
    )(codes, scales)


def finish(owned, expert, named, gate, up, h_ref, at, cols):
    which = lax.axis_index("expert") * owned + expert
    member = jnp.sum((named == which.astype(F32)).astype(F32), axis=1, keepdims=True)
    value = gate / (1.0 + jnp.exp(-gate)) * up
    h_ref[at, :, cols] = jnp.where(member > 0, value, 0.0).astype(BF16)
    return jnp.sum(member, keepdims=True)


def near_kernel(owned, mine_ref, theirs_ref, codes_ref, scale_ref, *refs):
    gate_refs, h_ref, count_ref = refs[:owned], refs[owned], refs[owned + 1]
    up_refs, x_ref = refs[-owned - 1 : -1], refs[-1]
    _, depth, width = codes_ref.shape
    groups = scale_ref.shape[1]
    step = depth // groups
    several = 2 if groups % 2 == 0 else 1
    labelled = jnp.concatenate([mine_ref[...], theirs_ref[...]])
    named = labelled[:, depth:].astype(F32)
    x_ref[...] = labelled[:, :depth]
    block = NEAR_BLOCK if width % NEAR_BLOCK == 0 else width
    for expert in range(owned):
        for col in range(0, width, block):
            cols = pl.ds(col, block)
            gate = jnp.dot(x_ref[...], gate_refs[expert][:, cols], preferred_element_type=F32)
            up = jnp.zeros(gate.shape, F32)
            for group in range(0, groups, several):
                part = pl.ds(group * step, several * step)
                codes = codes_ref[expert, part, cols].astype(F32).reshape(several, step, block)
                scale = scale_ref[expert, pl.ds(group, several), cols]
                w = (codes * scale[:, None, :]).astype(BF16).reshape(several * step, block)
                up_refs[expert][part, cols] = w
                up = up + jnp.dot(
                    x_ref[:, pl.ds(group * step, several * step)], w, preferred_element_type=F32
                )
            count = finish(owned, expert, named, gate, up, h_ref, expert, cols)
        count_ref[expert] = jnp.broadcast_to(count, count_ref.shape[1:])


def near_units(x, w_gate, up_codes, up_scales):
    owned, depth, width = up_codes.shape
    rows = sum(part.shape[0] for part in x)
    return pl.pallas_call(
        functools.partial(near_kernel, owned),
        in_specs=[pl.BlockSpec(memory_space=pltpu.VMEM)] * (4 + owned),
        out_specs=[pl.BlockSpec(memory_space=pltpu.VMEM)] * (2 + owned),
        out_shape=[
            jax.ShapeDtypeStruct((owned, rows, width), BF16),
            jax.ShapeDtypeStruct((owned, 32, LANES), F32),
        ]
        + [pltpu.VMEM((depth, width), BF16)] * owned,
        scratch_shapes=[pltpu.VMEM((rows, depth), BF16)],
        compiler_params=pltpu.CompilerParams(vmem_limit_bytes=2 << 20),
        cost_estimate=pl.CostEstimate(
            flops=1 << 33, bytes_accessed=4 * owned * depth * width, transcendentals=0
        ),
    )(*x, up_codes, up_scales, *w_gate)


def far_kernel(
    owned, expert, mine_ref, theirs_ref, gate_ref, up_ref, h_ref, count_ref, x_ref
):
    depth, width = gate_ref.shape
    labelled = jnp.concatenate([mine_ref[...], theirs_ref[...]])
    named = labelled[:, depth:].astype(F32)
    x_ref[...] = labelled[:, :depth]
    block = FAR_BLOCK if width % FAR_BLOCK == 0 else width
    for col in range(0, width, block):
        cols = pl.ds(col, block)
        gate = jnp.dot(x_ref[...], gate_ref[:, cols], preferred_element_type=F32)
        up = jnp.dot(x_ref[...], up_ref[:, cols], preferred_element_type=F32)
        count = finish(owned, expert, named, gate, up, h_ref, 0, cols)
    count_ref[0] = jnp.broadcast_to(count, count_ref.shape[1:])


def far_units(owned, expert, x, gate, up):
    depth, width = gate.shape
    rows = sum(part.shape[0] for part in x)
    return pl.pallas_call(
        functools.partial(far_kernel, owned, expert),
        in_specs=[pl.BlockSpec(memory_space=pltpu.VMEM)] * 4,
        out_specs=[pl.BlockSpec(memory_space=pltpu.VMEM)] * 2,
        out_shape=[
            jax.ShapeDtypeStruct((1, rows, width), BF16),
            jax.ShapeDtypeStruct((1, 32, LANES), F32),
        ],
        scratch_shapes=[pltpu.VMEM((rows, depth), BF16)],
        compiler_params=pltpu.CompilerParams(vmem_limit_bytes=2 << 20),
        cost_estimate=pl.CostEstimate(
            flops=4 * rows * depth * width,
            bytes_accessed=4 * depth * width,
            transcendentals=rows * width,
        ),
    )(*x, gate, up)


def gram_kernel(jobs, *refs):
    n = len(jobs)
    blocks = [refs[6 * i : 6 * i + 6] for i in range(n)]
    out_ref, buffer, sems = refs[-3:]
    me = lax.axis_index("dp")
    width = buffer.shape[2]
    size = width // PARTS
    copies = []
    for i, (expert, first, second, theirs) in enumerate(jobs):
        place = pl.ds(pl.multiple_of((1 - me if theirs else me) * width, LANES), width)
        left_a, left_b, right_a, right_b, count_a, count_b = blocks[i]
        left = jnp.concatenate([left_a[first], left_b[second]])
        if theirs:
            right = jnp.concatenate([right_b[second], right_a[first]])
        else:
            right = jnp.concatenate([right_a[first], right_b[second]])
        scale = 2.0 / (count_a[first, 0:1, 0:1] + count_b[second, 0:1, 0:1])
        for part in range(PARTS):
            rows = pl.ds(part * size, size)
            product = lax.dot_general(
                left[:, part * size : (part + 1) * size],
                right,
                (((0,), (0,)), ((), ())),
                preferred_element_type=F32,
            )
            buffer[i, rows, :] = product * scale
            copy = pltpu.make_async_copy(
                buffer.at[i, rows], out_ref.at[expert, rows, place], sems.at[i, part]
            )
            copy.start()
            copies.append(copy)
    for copy in copies:
        copy.wait()


def gram_blocks(jobs, operands, shape, onto=None):
    width = shape[1]
    n = len(jobs)
    flat = [x for group in operands for x in group]
    return pl.pallas_call(
        functools.partial(gram_kernel, jobs),
        in_specs=[pl.BlockSpec(memory_space=pltpu.VMEM)] * len(flat)
        + ([] if onto is None else [pl.BlockSpec(memory_space=pl.ANY)]),
        out_specs=pl.BlockSpec(memory_space=pl.ANY),
        out_shape=jax.ShapeDtypeStruct(shape, F32),
        input_output_aliases={} if onto is None else {len(flat): 0},
        scratch_shapes=[
            pltpu.VMEM((n, width, width), F32),
            pltpu.SemaphoreType.DMA((n, PARTS)),
        ],
        compiler_params=pltpu.CompilerParams(vmem_limit_bytes=8 << 20),
        cost_estimate=pl.CostEstimate(
            flops=2 * n * 128 * width * width,
            bytes_accessed=4 * n * width * width,
            transcendentals=0,
        ),
    )(*flat, *([] if onto is None else [onto]))


def paired(tokens, expert_ids, gate_codes, up_codes, gate_scales, up_scales):
    owned, _, width = gate_codes.shape
    owners = lax.axis_size("expert")
    every = tuple(range(owned))
    rows = label(tokens, expert_ids, 1 << 34)
    *w_gate, gate_done = weights(gate_codes, gate_scales)
    far_own = swap(rows, "dp")
    ring = [shift(rows, "expert", by) for by in range(2, owners, 2)]
    order = (0, 2, (1, 3), (3, 1))
    near, far_own = join([rows] + ring, [far_own, gate_done], order, keep=True)
    far_ring = swap(join(ring, [gate_done], (1, (0, 2))), "dp")
    near = (near, swap(near, "expert"))
    far_own, held = lax.optimization_barrier((far_own, near[1]))
    far_next = swap(far_own, "expert", 2)
    near = (near[0], held)
    near_hidden, near_count, *w_up = near_units(near, w_gate, up_codes, up_scales)
    far = join([far_own, far_ring, far_next], [near_count])
    far = (far, swap(far, "expert"))
    near_other = swap(near_hidden, "dp")
    far_parts = [far_units(owned, e, far, w_gate[e], w_up[e]) for e in every]
    far_other = [swap(hidden, "dp") for hidden, _ in far_parts]
    shape = (owned, width, 2 * width)
    own, other = [], []
    for e in every:
        hidden, count = far_parts[e]
        own.append((near_hidden, hidden, near_hidden, hidden, near_count, count))
        other.append((near_hidden, hidden, near_other, far_other[e], near_count, count))
    out = gram_blocks([(e, e, 0, False) for e in every], own, shape)
    for e in every:
        out = gram_blocks([(e, e, 0, True)], other[e : e + 1], shape, out)
    return out


def local(tokens, expert_ids, gate_codes, up_codes, gate_scales, up_scales):
    args = (tokens, expert_ids, gate_codes, up_codes, gate_scales, up_scales)
    owned, depth, width = gate_codes.shape
    fits = (
        lax.axis_size("dp") == 2
        and lax.axis_size("expert") == 8
        and width % (PARTS * LANES) == 0
        and depth % (16 * gate_scales.shape[1]) == 0
        and tokens.shape[0] * (lax.axis_size("expert") // 2) % 16 == 0
        and expert_ids.shape[1] <= LANES
        and owned * lax.axis_size("expert") <= 256
        and owned * depth * width * 4 <= 32 << 20
    )
    return paired(*args) if fits else general(*args)


def solution(mesh):
    return jax.shard_map(
        local,
        mesh=mesh,
        in_specs=(
            P(("groups", "expert", "dp"), None),
            P(("groups", "expert", "dp"), None),
            P("expert", None, "dp"),
            P("expert", None, "dp"),
            P("expert", None, "dp"),
            P("expert", None, "dp"),
        ),
        out_specs=P(("groups", "expert"), "dp", None),
        check_vma=False,
    )
```
